128 devices in a mesh: dp: 2 (over z_lo), fsdp: 64 (over y, z_hi, x, core).
Axes of the slice: x: 4, y: 4, z: 4 (z_hi: 2, z_lo: 2; z = z_hi * 2 + z_lo), core: 2. Of those that a mesh axis runs over, the one named last changes fastest.
Arguments:
- attention_out: bfloat16 [65536, 2560], P(('dp', 'fsdp')), may hold values from -24 to 24
- residual: bfloat16 [65536, 2560], P(('dp', 'fsdp')), may hold values from -6 to 6
- target_rows: bfloat16 [65536, 2560], P(('dp', 'fsdp')), may hold values from -0.125 to 0.125
- ref_logit: float32 [128, 512], P(('dp', 'fsdp')), may hold values from -9 to 9
- loss_weight: int32 [128, 512], P(('dp', 'fsdp')), may hold values from -2 to 2
- segment: int32 [128, 512], P(('dp', 'fsdp')), may hold values from 0 to 15, as said below
- counts: int32 [128], P(('dp', 'fsdp')), may hold values from 64 to 512, as said below
- out_weight: bfloat16 [2560, 2560], P('fsdp'), may hold values from -0.125 to 0.125
- norm_gain: float32 [2560], replicated, may hold values from 0.25 to 1.75
Outputs:
- grad_out_weight: float32 [2560, 2560], P('fsdp')
- grad_gain: float32 [2560], replicated
- grad_attention: bfloat16 [65536, 2560], P(('dp', 'fsdp'))
- loss: float32 [], replicated
The draws below stay inside these ranges and needn't reach their ends.
Inputs may be any that keep to these rules, and one draw needn't show every extreme that they name: `counts`: slots at or past a device's count are padding and carry no loss; at least one device is full. `segment`: is non-decreasing along each device's slots; documents do not cross devices.
All inputs are finite; a program needn't handle non-finite values.
Results may differ from the reference program's by a relative error of at most 0.0049.
Values may be sent and summed in bfloat16 or wider, within the bound.
A program may use at most 192 MiB of HBM per device.

```python
import jax
import jax.numpy as jnp
from jax import lax

DW = 2560
SEGS = 16
CAP = 512
HD = 2560
ROWS = 65536
DEVICES = 128


def draw_counts(key, part):
    key = jax.random.fold_in(key, 11)
    first_key, second_key = jax.random.split(key)
    drawn = jax.random.randint(first_key, (DEVICES,), CAP // 8, CAP // 2 + 1)
    chosen = jax.random.randint(second_key, (), 0, DEVICES)
    return jnp.where(jnp.arange(DEVICES) == chosen, CAP, drawn).astype(jnp.int32)


def draw_segment(key, part):
    key = jax.random.fold_in(key, 23)
    breaks = (jax.random.randint(key, (DEVICES, CAP), 0, 8) == 0).astype(jnp.int32)
    positions = jnp.arange(CAP)
    forced = (positions % (CAP // SEGS) == 0) & (positions > 0)
    breaks = jnp.where(forced[None, :], 1, breaks)
    breaks = jnp.where(positions[None, :] == 0, 0, breaks)
    return jnp.minimum(jnp.cumsum(breaks, axis=1), SEGS - 1).astype(jnp.int32)


def plant(values, key, low, high):
    longest = values.shape.index(max(values.shape))
    spots = []
    for shift in (0, 1):
        where = [jax.random.randint(jax.random.fold_in(key, axis), (), 0, length) for axis, length in enumerate(values.shape)]
        where[longest] = (where[longest] + shift) % values.shape[longest]
        spots.append(tuple(where))
    return values.at[spots[0]].set(low).at[spots[1]].set(high)


def strengthened(result, rng, source, target, parts, factor):
    def block_of(position):
        return (jnp.arange(result.shape[position]) // (result.shape[position] // parts)).reshape((-1,) + (1,) * (result.ndim - 1 - position))

    one_side = jax.random.permutation(rng, parts)[block_of(target)]
    second = (block_of(target) + parts // 2) % parts
    return jnp.where((block_of(source) == one_side) | (block_of(source) == second), factor * result, result)


def block_scale(stream_key, dims, cuts, low, top_value):
    factor_of = 1.0
    for dim, parts in cuts:
        heights = jax.random.uniform(jax.random.fold_in(jax.random.fold_in(stream_key, 6), dim), (parts,), jnp.float32, low / len(cuts), top_value / len(cuts))
        factor_of = factor_of * jnp.repeat(jnp.exp(heights), dims[dim] // parts).reshape((-1,) + (1,) * (len(dims) - 1 - dim))
    return factor_of


def normal_values(key, extent, spread, bound, pieces=(), kind=jnp.bfloat16):
    gain = block_scale(key, extent, pieces, -0.22, 0.18) if pieces else 1.0
    array = jax.random.normal(key, extent, jnp.float32) * spread * gain
    return jnp.minimum(jnp.maximum(array, -bound), bound).astype(kind)


def bell_draw_with(stream_key, dims, width, reach, cuts, heavy, held_as=jnp.bfloat16):
    values = width * jax.random.normal(stream_key, dims, jnp.float32)
    if cuts:
        values = values * block_scale(stream_key, dims, cuts, -0.22, 0.18)
    return jnp.clip(strengthened(values, jax.random.fold_in(stream_key, 3), *heavy), -reach, reach).astype(held_as)


def setup_inputs(seed: int = 0) -> dict:
    keys = jax.random.split(jax.random.key(seed), 10)
    return {
        "attention_out": bell_draw_with(keys[0], (ROWS, HD), 1.0, 24.0, ((0, 128),), (0, 1, 128, 5.5)),
        "residual": normal_values(keys[1], (ROWS, DW), 1.0, 6.0, ((0, 128),)),
        "target_rows": normal_values(keys[2], (ROWS, DW), DW ** -0.5, 0.125, ((0, 128),)),
        "ref_logit": normal_values(keys[3], (DEVICES, CAP), 1.5, 9.0, ((0, 128),), jnp.float32),
        "loss_weight": plant(jax.random.randint(keys[4], (DEVICES, CAP), -2, 3), jax.random.fold_in(keys[4], 1), -2, 2).astype(jnp.int32),
        "segment": draw_segment(jax.random.fold_in(keys[9], 71), 0),
        "counts": draw_counts(jax.random.fold_in(keys[9], 71), 0),
        "out_weight": normal_values(keys[7], (HD, DW), HD ** -0.5, 0.125, ((0, 64),)),
        "norm_gain": jnp.clip(1.0 + 0.15 * jax.random.normal(keys[8], (DW,), jnp.float32), 0.25, 1.75),
    }


npo_beta = 0.1
loss_scale = 1024.0

def local_pass(attention_rows, residual_rows, target, ref_row, weight_row, segment_row, out_weight, norm_gain, denominator):
    projected = jnp.dot(attention_rows, out_weight, preferred_element_type=jnp.float32)
    norm_scale = jnp.sqrt(lax.optimization_barrier(jnp.mean(projected * projected, axis=1, keepdims=True)) + 1e-06)
    normed = projected / norm_scale
    target_f = target.astype(jnp.float32)
    output_rows = residual_rows.astype(jnp.float32) + norm_gain[None, :] * normed
    target_score = lax.optimization_barrier(jnp.sum(output_rows * target_f, axis=1))
    forget_weight = jnp.maximum(-weight_row, 0).astype(jnp.float32)
    retain_weight = jnp.maximum(weight_row, 0).astype(jnp.float32)
    segment_table = (segment_row[:, None] == jnp.arange(SEGS, dtype=jnp.int32)[None, :]).astype(jnp.float32)
    seg_sum = jnp.dot(forget_weight * (target_score - ref_row), segment_table, precision=lax.Precision.HIGHEST)
    has_forget = jnp.dot(forget_weight, segment_table, precision=lax.Precision.HIGHEST) > 0.5
    npo_total = jnp.sum(jnp.where(has_forget, 2.0 / npo_beta * jax.nn.softplus(npo_beta * seg_sum), 0.0))
    loss_total = npo_total - jnp.sum(retain_weight * target_score)
    slot_sigmoid = jnp.dot(segment_table, jax.nn.sigmoid(npo_beta * seg_sum), precision=lax.Precision.HIGHEST)
    score_grad = loss_scale / denominator * (forget_weight * 2.0 * slot_sigmoid - retain_weight)
    output_grad = score_grad[:, None] * target_f
    gain_part = lax.optimization_barrier(jnp.sum(output_grad * normed, axis=0))
    normed_grad = output_grad * norm_gain[None, :]
    projected_grad = ((normed_grad - normed * lax.optimization_barrier(jnp.mean(normed_grad * normed, axis=1, keepdims=True))) / norm_scale).astype(jnp.bfloat16)
    grad_rows = lax.dot_general(projected_grad, out_weight, (((1,), (1,)), ((), ())), preferred_element_type=jnp.float32).astype(jnp.bfloat16)
    return (grad_rows, projected_grad, gain_part, loss_total)

def reference(attention_out, residual, target_rows, ref_logit, loss_weight, segment, counts, out_weight, norm_gain):
    live_slot = jnp.arange(CAP, dtype=jnp.int32)[None, :] < counts[:, None]
    clipped = jnp.where(live_slot, loss_weight, 0)
    denominator = jnp.maximum(jnp.sum(jnp.abs(clipped)).astype(jnp.float32), 1.0)
    stacked = (attention_out.reshape(DEVICES, CAP, HD), residual.reshape(DEVICES, CAP, DW), target_rows.reshape(DEVICES, CAP, DW), ref_logit, clipped, segment)

    def visit(carry, inputs):
        grad_weight, grad_norm, loss_sum = carry
        attention_rows, residual_rows, target, ref_row, weight_row, segment_row = inputs
        grad_rows, projected_grad, gain_part, loss_total = local_pass(attention_rows, residual_rows, target, ref_row, weight_row, segment_row, out_weight, norm_gain, denominator)
        grad_term = lax.dot_general(attention_rows, projected_grad, (((0,), (0,)), ((), ())), preferred_element_type=jnp.float32)
        return ((grad_weight + grad_term, grad_norm + gain_part, loss_sum + loss_total), grad_rows)
    start = (jnp.zeros((HD, DW), jnp.float32), jnp.zeros((DW,), jnp.float32), jnp.float32(0.0))
    (grad_weight, grad_norm, loss_sum), grad_rows = lax.scan(visit, start, stacked)
    return (grad_weight, grad_norm, grad_rows.reshape(DEVICES * CAP, HD), loss_sum / denominator)
```

```python
import functools

import jax
import jax.numpy as jnp
from jax import lax
from jax.experimental import pallas as pl
from jax.experimental.pallas import tpu as pltpu
from jax.sharding import PartitionSpec as P

SEGS = 16
F32 = jnp.float32
BF16 = jnp.bfloat16
MESH = pl.DeviceIdType.MESH

npo_beta = 0.1
loss_scale = 1024.0

ROW = 80
HALF = 40
CAP = 512
DW = 2560
HC = 1280
GW = 256
NG = HC // GW
WIDTH = (256, 256, 128)
ORDER = (0, 1, 3, 2)


def place():
    dp = lax.axis_index("dp")
    f = lax.axis_index("fsdp")
    return (f // 2) % 4, f // 16, ((f // 8) % 2) * 2 + dp, f % 2


def device(x, y, z, c):
    return (z % 2, ((y * 2 + z // 2) * 4 + x) * 2 + c)


def kernel(
    a_hbm,
    r_hbm,
    t_hbm,
    ref_ref,
    lw_ref,
    seg_ref,
    cnt_ref,
    w_ref,
    gain_ref,
    gw_out,
    gg_out,
    ga_out,
    loss_out,
    a2,
    at,
    t2,
    r2,
    wg,
    pr,
    pg,
    wx,
    meta,
    acc1,
    acc2,
    acc3,
    sp,
    alpha,
    beta,
    den,
    gsum,
    gsib,
    st_o0, st_o1, st_o2,
    st_n0, st_n1, st_n2,
    rl0, rl1, rl2,
    rv0, rv1, rv2,
    ow0, ow1, ow2,
    s20, s21, s22,
    v20, v21, v22,
    s30, s31, s32,
    v30, v31, v32,
    fb,
    fr,
    ga_send,
    ga_recv,
    ga_own,
    loc,
    sib_s, sib_r,
    den_s, den_r,
    g_s, g_r,
    p1_s, p1_r,
    p2_s, p2_r,
    p3_s, p3_r,
    p4_s, p4_r,
    q0_s, q0_r,
    q1_s, q1_r,
    q2_s, q2_r,
    q3_s, q3_r,
    qf_s, qf_r,
):
    st_o = (st_o0, st_o1, st_o2)
    st_n = (st_n0, st_n1, st_n2)
    rl = (rl0, rl1, rl2)
    rv = (rv0, rv1, rv2)
    own = (ow0, ow1, ow2)
    s2 = (s20, s21, s22)
    v2 = (v20, v21, v22)
    s3 = (s30, s31, s32)
    v3 = (v30, v31, v32)
    x, y, z, c = place()
    zl = z % 2
    sib = device(x, y, z, 1 - c)
    pieces = range(3)
    yz = (None, (1 - c, c), (c, 1 - c))

    def pos(p):
        if p == 0:
            return y, z, x
        m, n = yz[p]
        return x, z * m + y * n, y * m + z * n

    def coords(p, p1, p2, p3):
        if p == 0:
            return p3, p1, p2
        m, n = yz[p]
        return p1, p3 * m + p2 * n, p2 * m + p3 * n

    def peer(p, d1, d2, d3):
        p1, p2, p3 = pos(p)
        return device(*coords(p, (p1 + d1) % 4, (p2 + d2) % 4, (p3 + d3) % 4), c)

    def wslot(p, a3, a2_, start, n):
        bx, by, bz = coords(p, 0, a2_, a3)
        if p == 0:
            return wg.at[bz % 2, pl.ds(start, n), bz // 2, bx]
        if p == 1:
            return wg.at[2 + bz % 2, by, bz // 2, pl.ds(start, n)]
        return wg.at[4, by, bz // 2, pl.ds(start, n), :, pl.ds(pl.multiple_of((bz % 2) * 128, 128), 128)]

    def remote(src, dst, ss, rs, dev):
        return pltpu.make_async_remote_copy(
            src_ref=src, dst_ref=dst, send_sem=ss, recv_sem=rs, device_id=dev, device_id_type=MESH
        )

    mine = pl.ds(pl.multiple_of(c * HC, 128), HC)
    theirs = pl.ds(pl.multiple_of((1 - c) * HC, 128), HC)
    loads = [
        pltpu.make_async_copy(a_hbm, a2.at[0], loc.at[0]),
        pltpu.make_async_copy(t_hbm.at[:, mine], t2.at[0], loc.at[1]),
        pltpu.make_async_copy(r_hbm.at[:, mine], r2.at[0], loc.at[2]),
    ]
    for copy in loads:
        copy.start()

    partners = [sib, device(x, y, z + 1 - 2 * zl, 1 - c)]
    for d in (1, 2, 3):
        partners.append(device((x + d) % 4, y, z, c))
        partners.append(device(x, (y + d) % 4, z, c))
        partners.append(device(x, y, (z + d) % 4, c))
    barrier = pltpu.get_barrier_semaphore()
    for q in partners:
        pl.semaphore_signal(barrier, inc=1, device_id=q, device_id_type=MESH)

    lane = lax.broadcasted_iota(jnp.int32, (1, CAP), 1)
    live = lane < cnt_ref[0]
    weight = jnp.where(live, lw_ref[...], 0).astype(F32)
    magnitude = jnp.sum(jnp.abs(weight), axis=1, keepdims=True)
    rows8 = lax.broadcasted_iota(jnp.int32, (8, CAP), 0)
    meta[0] = jnp.where(
        rows8 == 0,
        jnp.broadcast_to(ref_ref[...], (8, CAP)),
        jnp.where(
            rows8 == 1,
            jnp.broadcast_to(weight, (8, CAP)),
            jnp.where(
                rows8 == 2,
                jnp.broadcast_to(seg_ref[...].astype(F32), (8, CAP)),
                jnp.broadcast_to(magnitude, (8, CAP)),
            ),
        ),
    )

    def shard_columns(core):
        base = core * HC
        return jnp.concatenate(
            [
                w_ref[:, pl.ds(pl.multiple_of(base + zl * 256, 128), 256)].astype(F32),
                w_ref[:, pl.ds(pl.multiple_of(base + 512 + zl * 256, 128), 256)].astype(F32),
                w_ref[:, pl.ds(pl.multiple_of(base + 1024 + zl * 128, 128), 128)].astype(F32),
            ],
            axis=1,
        )

    wx[0] = shard_columns(1 - c)
    pl.semaphore_wait(barrier, len(partners))

    sib_w = remote(wx.at[0], wx.at[1], sib_s.at[0], sib_r.at[0], sib)
    sib_m = remote(meta.at[0], meta.at[1], sib_s.at[1], sib_r.at[1], sib)
    sib_a = remote(a_hbm, a2.at[1], sib_s.at[2], sib_r.at[2], sib)
    sib_t = remote(t_hbm.at[:, theirs], t2.at[1], sib_s.at[3], sib_r.at[3], sib)
    sib_res = remote(r_hbm.at[:, theirs], r2.at[1], sib_s.at[4], sib_r.at[4], sib)
    for copy in (sib_w, sib_m, sib_a, sib_t, sib_res):
        copy.start()

    own_w = shard_columns(c)
    sib_w.wait_recv()
    got_w = wx[1]
    first = c == 0
    block = jnp.concatenate(
        [jnp.where(first, own_w, got_w), jnp.where(first, got_w, own_w)], axis=0
    ).astype(BF16)
    bx0, by0, bz0 = x, y, z // 2
    wg[zl, by0, bz0, bx0] = block[:, 0:256]
    wg[2 + zl, by0, bz0, bx0] = block[:, 256:512]
    wg[4, by0, bz0, bx0, :, pl.ds(pl.multiple_of(zl * 128, 128), 128)] = block[:, 512:640]

    ph1, ph2, ph3, ph4 = {}, {}, {}, {}
    for p in pieces:
        p1, p2, p3 = pos(p)
        for d in (1, 2, 3):
            slot = wslot(p, p3, p2, p1, 1)
            ph1[p, d] = remote(slot, slot, p1_s.at[p, d - 1], p1_r.at[p, d - 1], peer(p, d, 0, 0))
            line = wslot(p, p3, p2, 0, 4)
            ph2[p, d] = remote(line, line, p2_s.at[p, d - 1], p2_r.at[p, d - 1], peer(p, 0, d, 0))
        for d in range(4):
            a2_ = (p2 + d) % 4
            line = wslot(p, p3, a2_, 0, 4)
            low = wslot(p, (p3 + 3) % 4, a2_, 0, 2)
            high = wslot(p, (p3 + 1) % 4, a2_, 2, 2)
            ph3[p, d, 0] = remote(line, line, p3_s.at[p, d, 0], p3_r.at[p, d, 0], peer(p, 0, 0, 1))
            ph3[p, d, 1] = remote(line, line, p3_s.at[p, d, 1], p3_r.at[p, d, 1], peer(p, 0, 0, 3))
            ph4[p, d, 0] = remote(low, low, p4_s.at[p, d, 0], p4_r.at[p, d, 0], peer(p, 0, 0, 1))
            ph4[p, d, 1] = remote(high, high, p4_s.at[p, d, 1], p4_r.at[p, d, 1], peer(p, 0, 0, 3))

    sends = [sib_w, sib_m, sib_a, sib_t, sib_res]

    def start(copy):
        copy.start()
        sends.append(copy)

    for d in (1, 3, 2):
        for p in pieces:
            start(ph1[p, d])

    def den_phase(axis, value):
        at_ = (x, y, z)[axis]
        den[axis, at_] = value
        copies = []
        for d in (1, 2, 3):
            q = [x, y, z]
            q[axis] = (at_ + d) % 4
            slot = den.at[axis, at_]
            copy = remote(
                slot, slot, den_s.at[axis, d - 1], den_r.at[axis, d - 1], device(q[0], q[1], q[2], c)
            )
            start(copy)
            copies.append(copy)
        return copies

    def den_total(axis, copies):
        for copy in copies:
            copy.wait_recv()
        return den[axis, 0] + den[axis, 1] + den[axis, 2] + den[axis, 3]

    sib_m.wait_recv()
    den_copies = den_phase(0, meta[0, :, 0:128] * 0 + (meta[0, 3:4, 0:128] + meta[1, 3:4, 0:128]))

    def transpose_rows(slot):
        @pl.loop(0, DW // 128)
        def _(k):
            off = pl.ds(pl.multiple_of(k * 128, 128), 128)
            at[off, slot * CAP : (slot + 1) * CAP] = a2[slot, :, off].T

    for copy in loads:
        copy.wait()

    for p in pieces:
        for d in (1, 3, 2):
            ph1[p, d].wait_recv()
        for d in (1, 3, 2):
            start(ph2[p, d])
        start(ph3[p, 0, 0])
        start(ph3[p, 0, 1])

    den_copies = den_phase(1, den_total(0, den_copies))
    transpose_rows(0)

    for j in (1, 2, 3):
        d, before = ORDER[j], ORDER[j - 1]
        for p in pieces:
            ph2[p, 4 - d].wait_recv()
            start(ph3[p, d, 0])
            start(ph3[p, d, 1])
        for p in pieces:
            for s in (0, 1):
                ph3[p, before, s].wait_recv()
                start(ph4[p, before, s])
        if j == 1:
            den_copies = den_phase(2, den_total(1, den_copies))
            sib_a.wait_recv()
            transpose_rows(1)
        if j == 2:
            sib_t.wait_recv()
            sib_res.wait_recv()
            for slot in (0, 1):
                part = jnp.zeros((CAP, 128), F32)
                for k in range(HC // 128):
                    cols = slice(k * 128, (k + 1) * 128)
                    part += t2[slot, :, cols].astype(F32) * r2[slot, :, cols].astype(F32)
                acc2[slot] = part
            for slot in (0, 1):
                acc1[slot] = jnp.zeros((CAP, 128), F32)
                acc3[slot] = jnp.zeros((CAP, 128), F32)
    for p in pieces:
        for s in (0, 1):
            ph3[p, ORDER[3], s].wait_recv()
            start(ph4[p, ORDER[3], s])
    denominator = jnp.maximum(den_total(2, den_copies)[0:1, 0:1], 1.0)
    for p in pieces:
        for d in ORDER:
            for s in (0, 1):
                ph4[p, d, s].wait_recv()

    @pl.loop(0, NG)
    def _(g):
        cols = pl.ds(pl.multiple_of(g * GW, GW), GW)
        gains = gain_ref[:, pl.ds(pl.multiple_of(c * HC + g * GW, GW), GW)]
        w = wg[g].reshape(DW, GW)

        @pl.loop(0, 2)
        def _(slot):
            res = jnp.dot(a2[slot], w, preferred_element_type=F32)
            pr[g, slot] = res
            sq = res * res
            acc1[slot] += sq[:, :128] + sq[:, 128:]
            tp = res * t2[slot, :, cols].astype(F32) * gains
            acc3[slot] += tp[:, :128] + tp[:, 128:]

    lanes = lax.broadcasted_iota(jnp.int32, (CAP, 128), 1)

    @pl.loop(0, 2)
    def _(slot):
        q1 = jnp.sum(acc1[slot], axis=1, keepdims=True)
        q2 = jnp.sum(acc2[slot], axis=1, keepdims=True)
        q3 = jnp.sum(acc3[slot], axis=1, keepdims=True)
        sp[0, slot] = jnp.where(lanes == 0, q1, jnp.where(lanes == 1, q2, q3))

    stat = [
        remote(sp.at[0, s], sp.at[1, 1 - s], sib_s.at[5 + s], sib_r.at[5 + s], sib) for s in (0, 1)
    ]
    for copy in stat:
        start(copy)
    for copy in stat:
        copy.wait_recv()

    @pl.loop(0, 2)
    def _(slot):
        total = sp[0, slot] + sp[1, slot]
        q1, q2, q3 = total[:, 0:1], total[:, 1:2], total[:, 2:3]
        scale = jnp.sqrt(q1 * (1.0 / DW) + 1e-06)
        score = q2 + q3 / scale
        facts = meta[slot].T
        ref, wgt, seg = facts[:, 0:1], facts[:, 1:2], facts[:, 2:3]
        forget = jnp.maximum(-wgt, 0.0)
        retain = jnp.maximum(wgt, 0.0)
        table = (seg == lanes.astype(F32)).astype(F32)
        seg_sum = jnp.sum(table * (forget * (score - ref)), axis=0, keepdims=True)
        has = jnp.sum(table * forget, axis=0, keepdims=True) > 0.5
        scaled = npo_beta * seg_sum
        soft = jnp.maximum(scaled, 0.0) + jnp.log1p(jnp.exp(-jnp.abs(scaled)))
        npo = jnp.sum(jnp.where(has, 2.0 / npo_beta * soft, 0.0), axis=1, keepdims=True)
        loss = npo - jnp.sum(retain * score, axis=0, keepdims=True)

        @pl.when(slot == 0)
        def _():
            gsum[0, x] = jnp.zeros((8, HC + 128), F32)
            gsum[0, x, 0:1, HC : HC + 128] = jnp.broadcast_to(loss, (1, 128))

        sig = jnp.sum(table * jax.nn.sigmoid(scaled), axis=1, keepdims=True)
        grad = loss_scale / denominator * (forget * 2.0 * sig - retain)
        alpha[slot] = jnp.broadcast_to(grad / scale, (CAP, 128))
        beta[slot] = jnp.broadcast_to(q3 / (scale * scale * DW), (CAP, 128))

    @pl.loop(0, NG)
    def _(g):
        cols = pl.ds(pl.multiple_of(g * GW, GW), GW)
        gains = gain_ref[:, pl.ds(pl.multiple_of(c * HC + g * GW, GW), GW)]

        @pl.loop(0, 2)
        def _(slot):
            al = jnp.concatenate([alpha[slot], alpha[slot]], axis=1)
            be = jnp.concatenate([beta[slot], beta[slot]], axis=1)
            p_ = pr[g, slot]
            t = t2[slot, :, cols].astype(F32)
            rows = pl.ds(pl.multiple_of(slot * CAP, CAP), CAP)
            pg[g, rows] = (al * (t * gains - p_ * be)).astype(BF16)
            gsum[0, x, 0:1, cols] += jnp.sum(al * t * p_, axis=0, keepdims=True)

    def grad_blocks(p, v, emit):
        w_ = WIDTH[p]
        if p == 0:
            left = jnp.concatenate(
                [
                    at[pl.ds(pl.multiple_of((k * 4 + v) * ROW, 16), ROW), :] for k in range(8)
                ],
                axis=0,
            )
            for h in (0, 1):
                res = jnp.dot(left, pg[h], preferred_element_type=F32)
                for yy in range(4):
                    for zz in range(2):
                        k = yy * 2 + zz
                        emit(2 * zz + h, yy, res[k * ROW : (k + 1) * ROW])
            return
        m, n = yz[p]
        for h in (0, 1):
            parts = []
            for k in (0, 1):
                by = v * m + (2 * k + h) * n
                bz = k * m + (v // 2) * n
                parts.append(at[pl.ds(pl.multiple_of((by * 2 + bz) * 4 * ROW, 16), 4 * ROW), :])
            left = jnp.concatenate(parts, axis=0)
            side = h * m + (v % 2) * n
            if p == 1:
                right = pg[2 + side]
            else:
                right = pg[4, :, pl.ds(pl.multiple_of(side * 128, 128), 128)]
            res = jnp.dot(left, right, preferred_element_type=F32)
            for k in (0, 1):
                for xx in range(4):
                    i = k * 4 + xx
                    emit(2 * k + h, xx, res[i * ROW : (i + 1) * ROW])

    q0, q1, q2, q3 = {}, {}, {}, {}
    for p in pieces:
        p1, p2, p3 = pos(p)
        for s in (0, 1):
            half = pl.ds(2 * s, 2)
            to = peer(p, 0, 0, 1 + 2 * s)
            q0[p, s] = remote(st_o[p].at[:, half], rl[p].at[s], q0_s.at[p, s], q0_r.at[p, s], to)
            for d in range(4):
                i = (p2 + d) % 4
                q1[p, s, d] = remote(
                    st_n[p].at[s, i], rv[p].at[s, i], q1_s.at[p, s, d], q1_r.at[p, s, d], to
                )
        for d in (1, 2, 3):
            q2[p, d] = remote(
                s2[p].at[d - 1], v2[p].at[d - 1], q2_s.at[p, d - 1], q2_r.at[p, d - 1], peer(p, 0, d, 0)
            )
            q3[p, d] = remote(
                s3[p].at[d - 1], v3[p].at[d - 1], q3_s.at[p, d - 1], q3_r.at[p, d - 1], peer(p, d, 0, 0)
            )

    def put(ref, prefix=()):
        def emit(i, j, value):
            ref[prefix + (i, j)] = value.astype(ref.dtype)

        return emit

    for p in pieces:
        grad_blocks(p, (pos(p)[2] + 2) % 4, put(st_o[p]))
        start(q0[p, 0])
        start(q0[p, 1])

    def gain_phase(axis):
        at_ = (x, y, z)[axis]
        copies = []
        for d in (1, 2, 3):
            q = [x, y, z]
            q[axis] = (at_ + d) % 4
            slot = gsum.at[axis, at_]
            copy = remote(
                slot, slot, g_s.at[axis, d - 1], g_r.at[axis, d - 1], device(q[0], q[1], q[2], c)
            )
            start(copy)
            copies.append(copy)
        return copies

    def gain_total(axis, copies):
        for copy in copies:
            copy.wait_recv()
        return (gsum[axis, 0] + gsum[axis, 1]) + (gsum[axis, 2] + gsum[axis, 3])

    gain_copies = gain_phase(0)

    for p in pieces:
        grad_blocks(p, pos(p)[2], put(own[p]))

    gsum[1, y] = gain_total(0, gain_copies)
    gain_copies = gain_phase(1)

    for p in pieces:
        p2 = pos(p)[1]
        for s in (0, 1):
            q0[p, s].wait_recv()

            def emit(i, j, value, p=p, s=s):
                if j // 2 == s:
                    value = value + rl[p][s, i, j % 2].astype(F32)
                st_n[p][s, i, j] = value.astype(BF16)

            grad_blocks(p, (pos(p)[2] + 1 + 2 * s) % 4, emit)
            for d in (2, 1, 3, 0):
                start(q1[p, s, d])

    gsum[2, z] = gain_total(1, gain_copies)
    gain_copies = gain_phase(2)

    def grad_rows(slot, yy):
        res = jnp.zeros((CAP, 640), F32)
        for g in range(NG):
            w = wg[g, yy].reshape(640, GW)
            res = res + lax.dot_general(
                pg[g, slot * CAP : (slot + 1) * CAP],
                w,
                (((1,), (1,)), ((), ())),
                preferred_element_type=F32,
            )
        return res

    @pl.loop(0, 4)
    def _(yy):
        ga_send[:, pl.ds(pl.multiple_of(yy * 640, 128), 640)] = grad_rows(1, yy).astype(BF16)

    ga_copy = remote(ga_send, ga_recv, sib_s.at[7], sib_r.at[7], sib)
    start(ga_copy)

    def reduce_step(d):
        for p in pieces:
            p1, p2, p3 = pos(p)
            i = (p2 + d) % 4
            for s in (0, 1):
                q1[p, s, d].wait_recv()
            total = own[p][i] + rv[p][0, i].astype(F32) + rv[p][1, i].astype(F32)
            if d == 0:
                own[p][i] = total
            else:
                s2[p][d - 1] = total.astype(BF16)
                start(q2[p, d])

    reduce_step(2)
    reduce_step(1)

    ga_copy.wait_recv()

    @pl.loop(0, 4)
    def _(yy):
        cols = pl.ds(pl.multiple_of(yy * 640, 128), 640)
        ga_own[:, cols] = (grad_rows(0, yy) + ga_recv[:, cols].astype(F32)).astype(BF16)

    ga_store = pltpu.make_async_copy(ga_own, ga_out, loc.at[3])
    ga_store.start()

    reduce_step(3)
    reduce_step(0)

    total = gain_total(2, gain_copies)
    gsib[c] = total
    gcopy = remote(gsib.at[c], gsib.at[c], sib_s.at[8], sib_r.at[8], sib)
    start(gcopy)

    for p in pieces:
        p1, p2, p3 = pos(p)
        acc = own[p][p2]
        for d in (1, 3, 2):
            q2[p, d].wait_recv()
            acc = acc + v2[p][d - 1].astype(F32)
        own[p][p2] = acc
        for d in (1, 3, 2):
            s3[p][d - 1] = own[p][p2, (p1 + d) % 4].astype(BF16)
            start(q3[p, d])

    offs = (0, 256, 512)
    for p in pieces:
        p1, p2, p3 = pos(p)
        acc = own[p][p2, p1]
        for d in (1, 3, 2):
            q3[p, d].wait_recv()
            acc = acc + v3[p][d - 1].astype(F32)
        fb[:, offs[p] : offs[p] + WIDTH[p]] = acc

    keep = pl.ds(pl.multiple_of(c * HALF, 8), HALF)
    give = pl.ds(pl.multiple_of((1 - c) * HALF, 8), HALF)
    zn = z + 1 - 2 * zl
    last = [
        remote(fb.at[give], fr.at[0], qf_s.at[0], qf_r.at[0], sib),
        remote(fb.at[keep], fr.at[1], qf_s.at[1], qf_r.at[1], device(x, y, zn, c)),
        remote(fb.at[give], fr.at[2], qf_s.at[2], qf_r.at[2], device(x, y, zn, 1 - c)),
    ]
    for copy in (last[1], last[2], last[0]):
        start(copy)

    def place_columns(core, side, value):
        base = core * HC
        gw_out[:, pl.ds(pl.multiple_of(base + side * 256, 128), 256)] = value[:, 0:256]
        gw_out[:, pl.ds(pl.multiple_of(base + 512 + side * 256, 128), 256)] = value[:, 256:512]
        gw_out[:, pl.ds(pl.multiple_of(base + 1024 + side * 128, 128), 128)] = value[:, 512:640]

    place_columns(c, zl, fb[keep])

    gcopy.wait_recv()
    for core in (0, 1):
        gg_out[:, core * HC : (core + 1) * HC] = gsib[core, 0:1, 0:HC]
    loss_out[...] = (gsib[0, 0:1, HC : HC + 128] + gsib[1, 0:1, HC : HC + 128]) / denominator

    last[0].wait_recv()
    place_columns(1 - c, zl, fr[0])
    last[1].wait_recv()
    place_columns(c, 1 - zl, fr[1])
    last[2].wait_recv()
    place_columns(1 - c, 1 - zl, fr[2])

    for copy in sends:
        copy.wait_send()
    ga_store.wait()


def scratch():
    dma = pltpu.SemaphoreType.DMA
    vm = pltpu.VMEM
    out = [
        vm((2, CAP, DW), BF16),
        vm((DW, 2 * CAP), BF16),
        vm((2, CAP, HC), BF16),
        vm((2, CAP, HC), BF16),
        vm((NG, 4, 2, 4, ROW, GW), BF16),
        vm((NG, 2, CAP, GW), F32),
        vm((NG, 2 * CAP, GW), BF16),
        vm((2, HALF, 640), F32),
        vm((2, 8, CAP), F32),
        vm((2, CAP, 128), F32),
        vm((2, CAP, 128), F32),
        vm((2, CAP, 128), F32),
        vm((2, 2, CAP, 128), F32),
        vm((2, CAP, 128), F32),
        vm((2, CAP, 128), F32),
        vm((3, 4, 8, 128), F32),
        vm((3, 4, 8, HC + 128), F32),
        vm((2, 8, HC + 128), F32),
    ]
    out += [vm((4, 4, ROW, w), BF16) for w in WIDTH]
    out += [vm((2, 4, 4, ROW, w), BF16) for w in WIDTH]
    out += [vm((2, 4, 2, ROW, w), BF16) for w in WIDTH]
    out += [vm((2, 4, 4, ROW, w), BF16) for w in WIDTH]
    out += [vm((4, 4, ROW, w), F32) for w in WIDTH]
    out += [vm((3, 4, ROW, w), BF16) for w in WIDTH]
    out += [vm((3, 4, ROW, w), BF16) for w in WIDTH]
    out += [vm((3, ROW, w), BF16) for w in WIDTH]
    out += [vm((3, ROW, w), BF16) for w in WIDTH]
    out += [
        vm((ROW, 640), F32),
        vm((3, HALF, 640), F32),
        vm((CAP, DW), BF16),
        vm((CAP, DW), BF16),
        vm((CAP, DW), BF16),
        dma((4,)),
    ]
    for shape in ((9,), (3, 3), (3, 3), (3, 3), (3, 3), (3, 4, 2), (3, 4, 2), (3, 2), (3, 2, 4), (3, 3), (3, 3), (3,)):
        out += [dma(shape), dma(shape)]
    return out


def shards(attention_out, residual, target_rows, ref_logit, loss_weight, segment, counts, out_weight, norm_gain):
    any_ = pl.BlockSpec(memory_space=pl.ANY)
    vmem = pl.BlockSpec(memory_space=pltpu.VMEM)
    smem = pl.BlockSpec(memory_space=pltpu.SMEM)
    gw, gg, ga, loss = pl.pallas_call(
        kernel,
        out_shape=(
            jax.ShapeDtypeStruct((HALF, DW), F32),
            jax.ShapeDtypeStruct((1, DW), F32),
            jax.ShapeDtypeStruct((CAP, DW), BF16),
            jax.ShapeDtypeStruct((1, 128), F32),
        ),
        in_specs=[any_, any_, any_, vmem, vmem, vmem, smem, vmem, vmem],
        out_specs=(vmem, vmem, any_, vmem),
        scratch_shapes=scratch(),
        compiler_params=pltpu.CompilerParams(
            collective_id=0, has_side_effects=True, vmem_limit_bytes=62 * 2**20
        ),
        cost_estimate=pl.CostEstimate(
            flops=3 * 2 * CAP * DW * DW, bytes_accessed=4 * CAP * DW * 2, transcendentals=0
        ),
    )(
        attention_out,
        residual,
        target_rows,
        ref_logit,
        loss_weight,
        segment,
        counts,
        out_weight,
        norm_gain.reshape(1, DW),
    )
    return gw, gg.reshape(DW), ga, loss[0, 0]


def solution(mesh):
    rows = P(("dp", "fsdp"), None)
    placed = (rows,) * 6 + (P(("dp", "fsdp")), P("fsdp", None), P())
    return jax.shard_map(
        shards,
        mesh=mesh,
        in_specs=placed,
        out_specs=(P("fsdp", None), P(), rows, P()),
        check_vma=False,
    )
```

```python
import functools

import jax
import jax.numpy as jnp
from jax import lax
from jax.experimental import pallas as pl
from jax.experimental.pallas import tpu as pltpu
from jax.sharding import PartitionSpec as P

SEGS = 16
F32 = jnp.float32
BF16 = jnp.bfloat16
MESH = pl.DeviceIdType.MESH

npo_beta = 0.1
loss_scale = 1024.0

ROW = 80
HALF = 40
CAP = 512
DW = 2560
HC = 1280
GW = 256
NG = HC // GW
WIDTH = (256, 256, 128)
ORDER = (0, 1, 3, 2)
PARTS = 8


def place():
    dp = lax.axis_index("dp")
    f = lax.axis_index("fsdp")
    return (f // 2) % 4, f // 16, ((f // 8) % 2) * 2 + dp, f % 2


def device(x, y, z, c):
    return (z % 2, ((y * 2 + z // 2) * 4 + x) * 2 + c)


def kernel(
    a_hbm,
    r_hbm,
    t_hbm,
    ref_ref,
    lw_ref,
    seg_ref,
    cnt_ref,
    w_ref,
    gain_in,
    gw_out,
    gg_out,
    ga_out,
    loss_out,
    gain_row,
    gcol,
    a2,
    at,
    t2,
    r2,
    tt,
    wgp,
    wgn,
    pr,
    pg,
    wx,
    meta,
    stat,
    sp,
    alpha,
    beta,
    gacc,
    den,
    gsum,
    gsib,
    st_o0, st_o1, st_o2,
    st_n0, st_n1, st_n2,
    rl0, rl1, rl2,
    rv0, rv1, rv2,
    ow0, ow1, ow2,
    s20, s21, s22,
    v20, v21, v22,
    s30, s31, s32,
    v30, v31, v32,
    fb,
    fr,
    ga_send,
    ga_recv,
    ga_own,
    loc,
    sib_s, sib_r,
    den_s, den_r,
    g_s, g_r,
    p1_s, p1_r,
    p2_s, p2_r,
    p3_s, p3_r,
    p4_s, p4_r,
    q0_s, q0_r,
    qa_s, qa_r,
    q1_s, q1_r,
    q2_s, q2_r,
    q3_s, q3_r,
    qf_s, qf_r,
):
    st_o = (st_o0, st_o1, st_o2)
    st_n = (st_n0, st_n1, st_n2)
    rl = (rl0, rl1, rl2)
    rv = (rv0, rv1, rv2)
    own = (ow0, ow1, ow2)
    s2 = (s20, s21, s22)
    v2 = (v20, v21, v22)
    s3 = (s30, s31, s32)
    v3 = (v30, v31, v32)
    x, y, z, c = place()
    zl = z % 2
    sib = device(x, y, z, 1 - c)
    pieces = range(3)
    yz = ((1 - c, c), (1 - c, c), (c, 1 - c))

    def pos(p):
        m, n = yz[p]
        if p == 0:
            return y * m + z * n, z * m + y * n, x
        return x, z * m + y * n, y * m + z * n

    def coords(p, p1, p2, p3):
        m, n = yz[p]
        if p == 0:
            return p3, p1 * m + p2 * n, p2 * m + p1 * n
        return p1, p3 * m + p2 * n, p2 * m + p3 * n

    def peer(p, d1, d2, d3):
        p1, p2, p3 = pos(p)
        return device(*coords(p, (p1 + d1) % 4, (p2 + d2) % 4, (p3 + d3) % 4), c)

    def wslot(p, a3, a2_, start, n):
        if p == 0:
            return wgp.at[a2_, pl.ds(start, n), a3]
        bx, by, bz = coords(p, 0, a2_, a3)
        if p == 1:
            return wgn.at[bz % 2, by, bz // 2, pl.ds(start, n)]
        return wgn.at[2, by, bz // 2, pl.ds(start, n), :, pl.ds(pl.multiple_of((bz % 2) * 128, 128), 128)]

    def remote(src, dst, ss, rs, dev):
        return pltpu.make_async_remote_copy(
            src_ref=src, dst_ref=dst, send_sem=ss, recv_sem=rs, device_id=dev, device_id_type=MESH
        )

    mine = pl.ds(pl.multiple_of(c * HC, 128), HC)
    theirs = pl.ds(pl.multiple_of((1 - c) * HC, 128), HC)
    loads = [
        pltpu.make_async_copy(a_hbm, a2.at[0], loc.at[0]),
        pltpu.make_async_copy(t_hbm.at[:, mine], t2.at[0], loc.at[1]),
        pltpu.make_async_copy(r_hbm.at[:, mine], r2.at[0], loc.at[2]),
    ]
    for copy in loads:
        copy.start()

    partners = [sib, device(x, y, z + 1 - 2 * zl, 1 - c)]
    for d in (1, 2, 3):
        partners.append(device((x + d) % 4, y, z, c))
        partners.append(device(x, (y + d) % 4, z, c))
        partners.append(device(x, y, (z + d) % 4, c))
    barrier = pltpu.get_barrier_semaphore()
    for q in partners:
        pl.semaphore_signal(barrier, inc=1, device_id=q, device_id_type=MESH)

    lane = lax.broadcasted_iota(jnp.int32, (1, CAP), 1)
    live = lane < cnt_ref[0]
    weight = jnp.where(live, lw_ref[...], 0).astype(F32)
    magnitude = jnp.sum(jnp.abs(weight), axis=1, keepdims=True)
    rows8 = lax.broadcasted_iota(jnp.int32, (8, CAP), 0)
    meta[0] = jnp.where(
        rows8 == 0,
        jnp.broadcast_to(ref_ref[...], (8, CAP)),
        jnp.where(
            rows8 == 1,
            jnp.broadcast_to(weight, (8, CAP)),
            jnp.where(
                rows8 == 2,
                jnp.broadcast_to(seg_ref[...].astype(F32), (8, CAP)),
                jnp.broadcast_to(magnitude, (8, CAP)),
            ),
        ),
    )

    def shard_columns(core):
        base = core * HC
        return jnp.concatenate(
            [
                w_ref[:, pl.ds(pl.multiple_of(base + zl * 256, 128), 256)].astype(F32),
                w_ref[:, pl.ds(pl.multiple_of(base + 512 + zl * 256, 128), 256)].astype(F32),
                w_ref[:, pl.ds(pl.multiple_of(base + 1024 + zl * 128, 128), 128)].astype(F32),
            ],
            axis=1,
        )

    wx[0] = shard_columns(1 - c)
    gain_row[0, :] = gain_in[...]
    pl.semaphore_wait(barrier, len(partners))

    sib_w = remote(wx.at[0], wx.at[1], sib_s.at[0], sib_r.at[0], sib)
    sib_m = remote(meta.at[0], meta.at[1], sib_s.at[1], sib_r.at[1], sib)
    sib_a = remote(a_hbm, a2.at[1], sib_s.at[2], sib_r.at[2], sib)
    sib_t = remote(t_hbm.at[:, theirs], t2.at[1], sib_s.at[3], sib_r.at[3], sib)
    sib_res = remote(r_hbm.at[:, theirs], r2.at[1], sib_s.at[4], sib_r.at[4], sib)
    for copy in (sib_w, sib_m, sib_a, sib_t, sib_res):
        copy.start()

    own_w = shard_columns(c)
    sib_w.wait_recv()
    got_w = wx[1]
    first = c == 0
    block = jnp.concatenate(
        [jnp.where(first, own_w, got_w), jnp.where(first, got_w, own_w)], axis=0
    ).astype(BF16)
    bx0, by0, bz0 = x, y, z // 2
    wgp[pos(0)[1], pos(0)[0], x] = block[:, 0:256]
    wgn[zl, by0, bz0, bx0] = block[:, 256:512]
    wgn[2, by0, bz0, bx0, :, pl.ds(pl.multiple_of(zl * 128, 128), 128)] = block[:, 512:640]

    ph1, ph2, ph3, ph4 = {}, {}, {}, {}
    for p in pieces:
        p1, p2, p3 = pos(p)
        for d in (1, 2, 3):
            slot = wslot(p, p3, p2, p1, 1)
            ph1[p, d] = remote(slot, slot, p1_s.at[p, d - 1], p1_r.at[p, d - 1], peer(p, d, 0, 0))
            line = wslot(p, p3, p2, 0, 4)
            ph2[p, d] = remote(line, line, p2_s.at[p, d - 1], p2_r.at[p, d - 1], peer(p, 0, d, 0))
        for d in range(4):
            a2_ = (p2 + d) % 4
            line = wslot(p, p3, a2_, 0, 4)
            low = wslot(p, (p3 + 3) % 4, a2_, 0, 2)
            high = wslot(p, (p3 + 1) % 4, a2_, 2, 2)
            ph3[p, d, 0] = remote(line, line, p3_s.at[p, d, 0], p3_r.at[p, d, 0], peer(p, 0, 0, 1))
            ph3[p, d, 1] = remote(line, line, p3_s.at[p, d, 1], p3_r.at[p, d, 1], peer(p, 0, 0, 3))
            ph4[p, d, 0] = remote(low, low, p4_s.at[p, d, 0], p4_r.at[p, d, 0], peer(p, 0, 0, 1))
            ph4[p, d, 1] = remote(high, high, p4_s.at[p, d, 1], p4_r.at[p, d, 1], peer(p, 0, 0, 3))

    sends = [sib_w, sib_m, sib_a, sib_t, sib_res]

    def start(copy):
        copy.start()
        sends.append(copy)

    for d in (1, 3, 2):
        for p in pieces:
            start(ph1[p, d])

    def den_phase(axis, value):
        at_ = (x, y, z)[axis]
        den[axis, at_] = value
        copies = []
        for d in (1, 2, 3):
            q = [x, y, z]
            q[axis] = (at_ + d) % 4
            slot = den.at[axis, at_]
            copy = remote(
                slot, slot, den_s.at[axis, d - 1], den_r.at[axis, d - 1], device(q[0], q[1], q[2], c)
            )
            start(copy)
            copies.append(copy)
        return copies

    def den_total(axis, copies):
        for copy in copies:
            copy.wait_recv()
        return den[axis, 0] + den[axis, 1] + den[axis, 2] + den[axis, 3]

    sib_m.wait_recv()
    den_copies = den_phase(0, meta[0, :, 0:128] * 0 + (meta[0, 3:4, 0:128] + meta[1, 3:4, 0:128]))

    def transpose_rows(slot):
        @pl.loop(0, DW // 128)
        def _(k):
            off = pl.ds(pl.multiple_of(k * 128, 128), 128)
            at[off, slot * CAP : (slot + 1) * CAP] = a2[slot, :, off].T

    def transpose_targets(slot):
        @pl.loop(0, NG)
        def _(g):
            for k in (0, 1):
                off = pl.ds(pl.multiple_of(g * GW + k * 128, 128), 128)
                tt[g, k * 128 : (k + 1) * 128, slot * CAP : (slot + 1) * CAP] = t2[slot, :, off].T

    def slabs(p, v, h):
        m, n = yz[p]
        rows, weights = [], []
        if p == 0:
            for yy in range(4):
                for zz in range(2):
                    zc = 2 * zz + h
                    rows.append(at[pl.ds(pl.multiple_of(((yy * 2 + zz) * 4 + v) * ROW, 16), ROW), :])
                    weights.append(wgp[zc * m + yy * n, yy * m + zc * n, v])
            side = h
        else:
            side = h * m + (v % 2) * n
            for k in (0, 1):
                by = v * m + (2 * k + h) * n
                bz = k * m + (v // 2) * n
                rows.append(at[pl.ds(pl.multiple_of((by * 2 + bz) * 4 * ROW, 16), 4 * ROW), :])
                if p == 1:
                    weights.append(wgn[side, by, bz].reshape(4 * ROW, GW))
                else:
                    part = wgn[2, by, bz, :, :, pl.ds(pl.multiple_of(side * 128, 128), 128)]
                    weights.append(part.reshape(4 * ROW, 128))
        return jnp.concatenate(rows, axis=0), jnp.concatenate(weights, axis=0), side

    def forward(p, v):
        @pl.loop(0, 2)
        def _(h):
            rows, weights, side = slabs(p, v, h)
            res = lax.dot_general(weights, rows, (((0,), (0,)), ((), ())), preferred_element_type=F32)
            if p == 0:
                pr[side] += res
            elif p == 1:
                pr[2 + side] += res
            else:
                pr[4, pl.ds(pl.multiple_of(side * 128, 128), 128)] += res

    def last_place(p, d):
        return (pos(p)[2] + d) % 4

    gcol[...] = jnp.broadcast_to(
        gain_row[:, pl.ds(pl.multiple_of(c * HC, 128), HC)], (128, HC)
    ).T.reshape(NG, GW, 128)

    @pl.loop(0, NG)
    def _(g):
        pr[g] = jnp.zeros((GW, 2 * CAP), F32)

    for copy in loads:
        copy.wait()

    for p in pieces:
        for d in (1, 3, 2):
            ph1[p, d].wait_recv()
        for d in (1, 3, 2):
            start(ph2[p, d])
        if p == 0:
            start(ph3[p, 0, 0])
            start(ph3[p, 0, 1])
    for p in (1, 2):
        start(ph3[p, 0, 0])
        start(ph3[p, 0, 1])
    den_copies = den_phase(1, den_total(0, den_copies))

    def spread(p, d):
        ph2[p, 4 - d].wait_recv()
        start(ph3[p, d, 0])
        start(ph3[p, d, 1])

    def relay(p, d):
        for s in (0, 1):
            ph3[p, d, s].wait_recv()
            start(ph4[p, d, s])

    for d in (1, 3, 2):
        spread(0, d)
    transpose_rows(0)
    relay(0, 0)
    den_copies = den_phase(2, den_total(1, den_copies))
    sib_a.wait_recv()
    transpose_rows(1)
    for d in (1, 3, 2):
        spread(1, d)
        spread(2, d)
    relay(0, 1)
    forward(0, last_place(0, 0))
    sib_t.wait_recv()
    sib_res.wait_recv()
    for slot in (0, 1):
        part = jnp.zeros((CAP, 128), F32)
        for k in range(HC // 128):
            cols = slice(k * 128, (k + 1) * 128)
            part += t2[slot, :, cols].astype(F32) * r2[slot, :, cols].astype(F32)
        sp[0, slot] = jnp.broadcast_to(jnp.sum(part.T, axis=0, keepdims=True), (8, CAP))
    relay(1, 0)
    relay(2, 0)
    relay(0, 3)
    transpose_targets(0)
    forward(1, last_place(1, 0))
    forward(2, last_place(2, 0))
    relay(1, 1)
    relay(2, 1)
    relay(0, 2)
    transpose_targets(1)
    forward(0, last_place(0, 1))
    forward(0, last_place(0, 3))
    for d in (3, 2):
        relay(1, d)
        relay(2, d)
    for p in (1, 2):
        for d in (1, 3):
            forward(p, last_place(p, d))
    denominator = jnp.maximum(den_total(2, den_copies)[0:1, 0:1], 1.0)
    for p in pieces:
        for d in ORDER:
            for s in (0, 1):
                ph4[p, d, s].wait_recv()
        forward(p, last_place(p, 2))

    stat[...] = jnp.zeros((2, 8, 2 * CAP), F32)

    @pl.loop(0, NG)
    def _(g):
        for slot in (0, 1):
            cols = slice(slot * CAP, (slot + 1) * CAP)
            gains = jnp.concatenate([gcol[g]] * 4, axis=1)
            p_ = pr[g, :, cols]
            stat[0, :, cols] += jnp.sum((p_ * p_).reshape(GW // 8, 8, CAP), axis=0)
            tp = p_ * tt[g, :, cols].astype(F32) * gains
            stat[1, :, cols] += jnp.sum(tp.reshape(GW // 8, 8, CAP), axis=0)

    row = lax.broadcasted_iota(jnp.int32, (8, CAP), 0)
    for slot in (0, 1):
        cols = slice(slot * CAP, (slot + 1) * CAP)
        q1 = jnp.sum(stat[0, :, cols], axis=0, keepdims=True)
        q3 = jnp.sum(stat[1, :, cols], axis=0, keepdims=True)
        sp[0, slot] = jnp.where(row == 0, q1, jnp.where(row == 1, q3, sp[0, slot]))

    swap = [
        remote(sp.at[0, s], sp.at[1, 1 - s], sib_s.at[5 + s], sib_r.at[5 + s], sib) for s in (0, 1)
    ]
    for copy in swap:
        start(copy)
    for copy in swap:
        copy.wait_recv()

    segs = lax.broadcasted_iota(jnp.int32, (SEGS, CAP), 0).astype(F32)
    gsum[0, x] = jnp.zeros((8, HC + 128), F32)
    for slot in (0, 1):
        total = sp[0, slot] + sp[1, slot]
        q1, q3, q2 = total[0:1], total[1:2], total[2:3]
        scale = jnp.sqrt(q1 * (1.0 / DW) + 1e-06)
        score = q2 + q3 / scale
        ref, wgt, seg = meta[slot, 0:1], meta[slot, 1:2], meta[slot, 2:3]
        forget = jnp.maximum(-wgt, 0.0)
        retain = jnp.maximum(wgt, 0.0)
        table = (seg == segs).astype(F32)
        seg_sum = jnp.sum(table * (forget * (score - ref)), axis=1, keepdims=True)
        has = jnp.sum(table * forget, axis=1, keepdims=True) > 0.5
        scaled = npo_beta * seg_sum
        if slot == 0:
            soft = jnp.maximum(scaled, 0.0) + jnp.log1p(jnp.exp(-jnp.abs(scaled)))
            npo = jnp.sum(jnp.where(has, 2.0 / npo_beta * soft, 0.0), axis=0, keepdims=True)
            loss = npo - jnp.sum(retain * score, axis=1, keepdims=True)
            gsum[0, x, 0:1, HC : HC + 128] = jnp.broadcast_to(loss, (1, 128))
        sig = jnp.sum(table * jax.nn.sigmoid(scaled), axis=0, keepdims=True)
        grad = loss_scale / denominator * (forget * 2.0 * sig - retain)
        alpha[slot] = jnp.broadcast_to(grad / scale, (8, CAP))
        beta[slot] = jnp.broadcast_to(q3 / (scale * scale * DW), (8, CAP))

    @pl.loop(0, NG)
    def _(g):
        gains = jnp.concatenate([gcol[g]] * 4, axis=1)
        part = jnp.zeros((GW, 128), F32)
        for slot in (0, 1):
            cols = slice(slot * CAP, (slot + 1) * CAP)
            al, be = alpha[slot, 0:1], beta[slot, 0:1]
            p_ = pr[g, :, cols]
            t = tt[g, :, cols].astype(F32)
            pg[g, :, cols] = (al * (t * gains - p_ * be)).astype(BF16)
            u = al * t * p_
            part += (u[:, 0:128] + u[:, 128:256]) + (u[:, 256:384] + u[:, 384:512])
        gacc[g] = part

    @pl.loop(0, NG)
    def _(g):
        cols = pl.ds(pl.multiple_of(g * GW, GW), GW)
        gsum[0, x, 0:1, cols] = jnp.sum(gacc[g].T, axis=0, keepdims=True)

    def grad_blocks(p, v, emit):
        m, n = yz[p]
        for h in (0, 1):
            rows, _, side = slabs(p, v, h)
            if p == 2:
                right = pg[4, pl.ds(pl.multiple_of(side * 128, 128), 128)]
            else:
                right = pg[2 * p + side]
            res = lax.dot_general(rows, right, (((1,), (1,)), ((), ())), preferred_element_type=F32)
            for k in range(8):
                value = res[k * ROW : (k + 1) * ROW]
                if p == 0:
                    yy, zc = k // 2, 2 * (k % 2) + h
                    emit(zc * m + yy * n, yy * m + zc * n, value)
                else:
                    emit(2 * (k // 4) + h, k % 4, value)

    q0, qa, q1, q2, q3 = {}, {}, {}, {}, {}
    for p in pieces:
        p1, p2, p3 = pos(p)
        for s in (0, 1):
            half = pl.ds(2 * s, 2)
            to = peer(p, 0, 0, 1 + 2 * s)
            q0[p, s] = remote(st_o[p].at[:, half], rl[p].at[s], q0_s.at[p, s], q0_r.at[p, s], to)
            free = pl.ds(2 * (1 - s), 2)
            qa[p, s] = remote(
                st_n[p].at[s, :, free], rv[p].at[s, :, free], qa_s.at[p, s], qa_r.at[p, s], to
            )
            for d in range(4):
                i = (p2 + d) % 4
                q1[p, s, d] = remote(
                    st_n[p].at[s, i, half], rv[p].at[s, i, half], q1_s.at[p, s, d], q1_r.at[p, s, d], to
                )
        for d in (1, 2, 3):
            q2[p, d] = remote(
                s2[p].at[d - 1], v2[p].at[d - 1], q2_s.at[p, d - 1], q2_r.at[p, d - 1], peer(p, 0, d, 0)
            )
            q3[p, d] = remote(
                s3[p].at[d - 1], v3[p].at[d - 1], q3_s.at[p, d - 1], q3_r.at[p, d - 1], peer(p, d, 0, 0)
            )

    def put(ref, prefix=()):
        def emit(i, j, value):
            ref[prefix + (i, j)] = value.astype(ref.dtype)

        return emit

    for p in pieces:
        grad_blocks(p, (pos(p)[2] + 2) % 4, put(st_o[p]))
        start(q0[p, 0])
        start(q0[p, 1])

    def gain_phase(axis):
        at_ = (x, y, z)[axis]
        copies = []
        for d in (1, 2, 3):
            q = [x, y, z]
            q[axis] = (at_ + d) % 4
            slot = gsum.at[axis, at_]
            copy = remote(
                slot, slot, g_s.at[axis, d - 1], g_r.at[axis, d - 1], device(q[0], q[1], q[2], c)
            )
            start(copy)
            copies.append(copy)
        return copies

    def gain_total(axis, copies):
        for copy in copies:
            copy.wait_recv()
        return (gsum[axis, 0] + gsum[axis, 1]) + (gsum[axis, 2] + gsum[axis, 3])

    gain_copies = gain_phase(0)

    for p in pieces:
        for t_ in (0, 1):
            grad_blocks(p, (pos(p)[2] + 1 + 2 * t_) % 4, put(st_n[p], (t_,)))
            start(qa[p, t_])

    gsum[1, y] = gain_total(0, gain_copies)
    gain_copies = gain_phase(1)

    for p in pieces:
        grad_blocks(p, pos(p)[2], put(own[p]))

    for p in (1, 2, 0):
        for d in (2, 1, 3, 0):
            i = (pos(p)[1] + d) % 4
            for t_ in (0, 1):
                if d == 2:
                    q0[p, t_].wait_recv()
                half = slice(2 * t_, 2 * t_ + 2)
                both = st_n[p][t_, i, half].astype(F32) + rl[p][t_, i].astype(F32)
                st_n[p][t_, i, half] = both.astype(BF16)
                start(q1[p, t_, d])

    gsum[2, z] = gain_total(1, gain_copies)
    gain_copies = gain_phase(2)

    def lines(h, yy):
        m, n = yz[0]
        out = []
        for zz in range(2):
            zc = 2 * zz + h
            out.append(wgp[zc * m + yy * n, yy * m + zc * n].reshape(4 * ROW, GW))
        return jnp.concatenate(out, axis=0)

    def grad_rows(slot, yy):
        res = jnp.zeros((640, CAP), F32)
        for g in range(NG):
            w = lines(g, yy) if g < 2 else wgn[g - 2, yy].reshape(640, GW)
            right = pg[g, :, slot * CAP : (slot + 1) * CAP]
            res = res + jnp.dot(w, right, preferred_element_type=F32)
        return res

    @pl.loop(0, 4)
    def _(yy):
        ga_send[pl.ds(pl.multiple_of(yy * 640, 128), 640), :] = grad_rows(1, yy).astype(BF16)

    ga_copy = remote(ga_send, ga_recv, sib_s.at[7], sib_r.at[7], sib)
    start(ga_copy)

    def reduce_step(p, d):
        p1, p2, p3 = pos(p)
        i = (p2 + d) % 4
        for t_ in (0, 1):
            if d == 2:
                qa[p, t_].wait_recv()
            q1[p, t_, d].wait_recv()
        total = own[p][i] + rv[p][0, i].astype(F32) + rv[p][1, i].astype(F32)
        if d == 0:
            own[p][i] = total
        else:
            s2[p][d - 1] = total.astype(BF16)
            start(q2[p, d])

    reduce_step(1, 2)
    reduce_step(2, 2)
    reduce_step(1, 1)
    reduce_step(2, 1)

    ga_copy.wait_recv()

    @pl.loop(0, 4)
    def _(yy):
        rows = pl.ds(pl.multiple_of(yy * 640, 128), 640)
        both = (grad_rows(0, yy) + ga_recv[rows, :].astype(F32)).astype(BF16)
        for k in range(5):
            cols = pl.ds(pl.multiple_of(yy * 640 + k * 128, 128), 128)
            ga_own[:, cols] = both[k * 128 : (k + 1) * 128].T

    ga_store = pltpu.make_async_copy(ga_own, ga_out, loc.at[3])
    ga_store.start()

    for p, d in ((1, 3), (2, 3), (0, 2), (1, 0), (2, 0)):
        reduce_step(p, d)

    def second(p):
        p1, p2, p3 = pos(p)
        acc = own[p][p2]
        for d in (1, 3, 2):
            q2[p, d].wait_recv()
            acc = acc + v2[p][d - 1].astype(F32)
        own[p][p2] = acc
        for d in (1, 3, 2):
            s3[p][d - 1] = own[p][p2, (p1 + d) % 4].astype(BF16)
            start(q3[p, d])

    offs = (0, 256, 512)
    keep = pl.ds(pl.multiple_of(c * HALF, 8), HALF)
    give = pl.ds(pl.multiple_of((1 - c) * HALF, 8), HALF)
    zn = z + 1 - 2 * zl
    last = {}

    def third(p):
        p1, p2, p3 = pos(p)
        acc = own[p][p2, p1]
        for d in (1, 3, 2):
            q3[p, d].wait_recv()
            acc = acc + v3[p][d - 1].astype(F32)
        cols = slice(offs[p], offs[p] + WIDTH[p])
        fb[:, cols] = acc
        last[p] = [
            remote(fb.at[give, cols], fr.at[0, :, cols], qf_s.at[p, 0], qf_r.at[p, 0], sib),
            remote(fb.at[keep, cols], fr.at[1, :, cols], qf_s.at[p, 1], qf_r.at[p, 1], device(x, y, zn, c)),
            remote(fb.at[give, cols], fr.at[2, :, cols], qf_s.at[p, 2], qf_r.at[p, 2], device(x, y, zn, 1 - c)),
        ]
        for copy in (last[p][1], last[p][2], last[p][0]):
            start(copy)

    reduce_step(0, 1)
    second(1)
    second(2)
    reduce_step(0, 3)
    reduce_step(0, 0)
    second(0)

    total = gain_total(2, gain_copies)
    gsib[c] = total
    gcopy = remote(gsib.at[c], gsib.at[c], sib_s.at[8], sib_r.at[8], sib)
    start(gcopy)

    third(1)
    third(2)
    third(0)

    def place_columns(core, side, value):
        base = core * HC
        gw_out[:, pl.ds(pl.multiple_of(base + side * 256, 128), 256)] = value[:, 0:256]
        gw_out[:, pl.ds(pl.multiple_of(base + 512 + side * 256, 128), 256)] = value[:, 256:512]
        gw_out[:, pl.ds(pl.multiple_of(base + 1024 + side * 128, 128), 128)] = value[:, 512:640]

    place_columns(c, zl, fb[keep])

    gcopy.wait_recv()
    for core in (0, 1):
        gg_out[:, core * HC : (core + 1) * HC] = gsib[core, 0:1, 0:HC]
    loss_out[...] = (gsib[0, 0:1, HC : HC + 128] + gsib[1, 0:1, HC : HC + 128]) / denominator

    for p in (1, 2, 0):
        for copy in last[p]:
            copy.wait_recv()
    place_columns(1 - c, zl, fr[0])
    place_columns(c, 1 - zl, fr[1])
    place_columns(1 - c, 1 - zl, fr[2])

    for copy in sends:
        copy.wait_send()
    ga_store.wait()


def scratch():
    dma = pltpu.SemaphoreType.DMA
    vm = pltpu.VMEM
    out = [
        vm((1, DW), F32),
        vm((NG, GW, 128), F32),
        vm((2, CAP, DW), BF16),
        vm((DW, 2 * CAP), BF16),
        vm((2, CAP, HC), BF16),
        vm((2, CAP, HC), BF16),
        vm((NG, GW, 2 * CAP), BF16),
        vm((4, 4, 4, ROW, GW), BF16),
        vm((NG - 2, 4, 2, 4, ROW, GW), BF16),
        vm((NG, GW, 2 * CAP), F32),
        vm((NG, GW, 2 * CAP), BF16),
        vm((2, HALF, 640), F32),
        vm((2, 8, CAP), F32),
        vm((2, 8, 2 * CAP), F32),
        vm((2, 2, 8, CAP), F32),
        vm((2, 8, CAP), F32),
        vm((2, 8, CAP), F32),
        vm((NG, GW, 128), F32),
        vm((3, 4, 8, 128), F32),
        vm((3, 4, 8, HC + 128), F32),
        vm((2, 8, HC + 128), F32),
    ]
    out += [vm((4, 4, ROW, w), BF16) for w in WIDTH]
    out += [vm((2, 4, 4, ROW, w), BF16) for w in WIDTH]
    out += [vm((2, 4, 2, ROW, w), BF16) for w in WIDTH]
    out += [vm((2, 4, 4, ROW, w), BF16) for w in WIDTH]
    out += [vm((4, 4, ROW, w), F32) for w in WIDTH]
    out += [vm((3, 4, ROW, w), BF16) for w in WIDTH]
    out += [vm((3, 4, ROW, w), BF16) for w in WIDTH]
    out += [vm((3, ROW, w), BF16) for w in WIDTH]
    out += [vm((3, ROW, w), BF16) for w in WIDTH]
    out += [
        vm((ROW, 640), F32),
        vm((3, HALF, 640), F32),
        vm((DW, CAP), BF16),
        vm((DW, CAP), BF16),
        vm((CAP, DW), BF16),
        dma((4,)),
    ]
    for shape in ((9,), (3, 3), (3, 3), (3, 3), (3, 3), (3, 4, 2), (3, 4, 2), (3, 2), (3, 2), (3, 2, 4), (3, 3), (3, 3), (3, 3)):
        out += [dma(shape), dma(shape)]
    return out


def finish(gw, gg, ga, loss, gw_out, gg_out, ga_out, loss_out, gw_v, ga_v, s_in, s_out):
    n = CAP // PARTS
    pairs = [(gw, gw_v, gw_out)]
    for k in range(PARTS):
        rows = slice(k * n, (k + 1) * n)
        pairs.append((ga.at[rows], ga_v.at[rows], ga_out.at[rows]))
    loads = [pltpu.make_async_copy(src, mid, s_in.at[i]) for i, (src, mid, _) in enumerate(pairs)]
    stores = [pltpu.make_async_copy(mid, dst, s_out.at[i]) for i, (_, mid, dst) in enumerate(pairs)]
    for copy in loads:
        copy.start()
    gg_out[...] = gg[0, :]
    loss_out[0, 0] = loss[0, 0]
    for load, store in zip(loads, stores):
        load.wait()
        store.start()
    for copy in stores:
        copy.wait()


def shards(attention_out, residual, target_rows, ref_logit, loss_weight, segment, counts, out_weight, norm_gain):
    any_ = pl.BlockSpec(memory_space=pl.ANY)
    vmem = pl.BlockSpec(memory_space=pltpu.VMEM)
    smem = pl.BlockSpec(memory_space=pltpu.SMEM)
    gw, gg, ga, loss = pl.pallas_call(
        kernel,
        out_shape=(
            jax.ShapeDtypeStruct((HALF, DW), F32),
            jax.ShapeDtypeStruct((1, DW), F32),
            jax.ShapeDtypeStruct((CAP, DW), BF16),
            jax.ShapeDtypeStruct((1, 128), F32),
        ),
        in_specs=[any_, any_, any_, vmem, vmem, vmem, smem, vmem, vmem],
        out_specs=(vmem, vmem, any_, vmem),
        scratch_shapes=scratch(),
        compiler_params=pltpu.CompilerParams(
            collective_id=0, has_side_effects=True, vmem_limit_bytes=62 * 2**20
        ),
        cost_estimate=pl.CostEstimate(
            flops=3 * 2 * CAP * DW * DW, bytes_accessed=4 * CAP * DW * 2, transcendentals=0
        ),
    )(
        attention_out,
        residual,
        target_rows,
        ref_logit,
        loss_weight,
        segment,
        counts,
        out_weight,
        norm_gain,
    )
    gw, gg, ga, loss = pl.pallas_call(
        finish,
        out_shape=(
            jax.ShapeDtypeStruct((HALF, DW), F32),
            jax.ShapeDtypeStruct((DW,), F32),
            jax.ShapeDtypeStruct((CAP, DW), BF16),
            jax.ShapeDtypeStruct((1, 1), F32),
        ),
        in_specs=[any_, vmem, any_, vmem],
        out_specs=(any_, vmem, any_, smem),
        scratch_shapes=[
            pltpu.VMEM((HALF, DW), F32),
            pltpu.VMEM((CAP, DW), BF16),
            pltpu.SemaphoreType.DMA((PARTS + 1,)),
            pltpu.SemaphoreType.DMA((PARTS + 1,)),
        ],
        compiler_params=pltpu.CompilerParams(vmem_limit_bytes=62 * 2**20),
    )(gw, gg, ga, loss)
    return gw, gg, ga, loss[0, 0]


def solution(mesh):
    rows = P(("dp", "fsdp"), None)
    placed = (rows,) * 6 + (P(("dp", "fsdp")), P("fsdp", None), P())
    return jax.shard_map(
        shards,
        mesh=mesh,
        in_specs=placed,
        out_specs=(P("fsdp", None), P(), rows, P()),
        check_vma=False,
    )
```

```python
import functools

import jax
import jax.numpy as jnp
from jax import lax
from jax.experimental import pallas as pl
from jax.experimental.pallas import tpu as pltpu
from jax.sharding import PartitionSpec as P

SEGS = 16
F32 = jnp.float32
BF16 = jnp.bfloat16
MESH = pl.DeviceIdType.MESH

npo_beta = 0.1
loss_scale = 1024.0

ROW = 80
HALF = 40
PAD = 48
CAP = 512
DW = 2560
HC = 1280
GW = 256
NG = HC // GW
WIDTH = (256, 256, 128)
ORDER = (0, 1, 3, 2)
PARTS = 8


def place():
    dp = lax.axis_index("dp")
    f = lax.axis_index("fsdp")
    return (f // 2) % 4, f // 16, ((f // 8) % 2) * 2 + dp, f % 2


def device(x, y, z, c):
    return (z % 2, ((y * 2 + z // 2) * 4 + x) * 2 + c)


def kernel(
    a_hbm,
    r_hbm,
    t_hbm,
    ref_ref,
    lw_ref,
    seg_ref,
    cnt_ref,
    w_ref,
    gain_in,
    gw_out,
    gg_out,
    ga_out,
    loss_out,
    gain_row,
    gcol,
    a2,
    at,
    t2,
    r2,
    tt,
    wgp,
    wgn,
    pr,
    pg,
    wx,
    meta,
    stat,
    sp,
    alpha,
    beta,
    gacc,
    den,
    gsum,
    gsib,
    st_o0, st_o1, st_o2,
    st_n0, st_n1, st_n2,
    rl0, rl1, rl2,
    rv0, rv1, rv2,
    ow0, ow1, ow2,
    s20, s21, s22,
    v20, v21, v22,
    w20, w21, w22,
    s30, s31, s32,
    v30, v31, v32,
    fb,
    fr,
    ga_send,
    ga_recv,
    ga_own,
    loc,
    sib_s, sib_r,
    den_s, den_r,
    g_s, g_r,
    p1_s, p1_r,
    p2_s, p2_r,
    p3_s, p3_r,
    p4_s, p4_r,
    q0_s, q0_r,
    qa_s, qa_r,
    q1_s, q1_r,
    q2_s, q2_r,
    q3_s, q3_r,
    qf_s, qf_r,
    ga_s, ga_r,
):
    st_o = (st_o0, st_o1, st_o2)
    st_n = (st_n0, st_n1, st_n2)
    rl = (rl0, rl1, rl2)
    rv = (rv0, rv1, rv2)
    own = (ow0, ow1, ow2)
    s2 = (s20, s21, s22)
    v2 = (v20, v21, v22)
    w2 = (w20, w21, w22)
    s3 = (s30, s31, s32)
    v3 = (v30, v31, v32)
    x, y, z, c = place()
    zl = z % 2
    sib = device(x, y, z, 1 - c)
    pieces = range(3)
    yz = ((1 - c, c), (1 - c, c), (c, 1 - c))

    def pos(p):
        m, n = yz[p]
        if p == 0:
            return y * m + z * n, z * m + y * n, x
        return x, z * m + y * n, y * m + z * n

    def coords(p, p1, p2, p3):
        m, n = yz[p]
        if p == 0:
            return p3, p1 * m + p2 * n, p2 * m + p1 * n
        return p1, p3 * m + p2 * n, p2 * m + p3 * n

    def peer(p, d1, d2, d3):
        p1, p2, p3 = pos(p)
        return device(*coords(p, (p1 + d1) % 4, (p2 + d2) % 4, (p3 + d3) % 4), c)

    def wslot(p, a3, a2_, start, n):
        if p == 0:
            return wgp.at[a2_, pl.ds(start, n), a3]
        bx, by, bz = coords(p, 0, a2_, a3)
        if p == 1:
            return wgn.at[bz % 2, by, bz // 2, pl.ds(start, n)]
        return wgn.at[2, by, bz // 2, pl.ds(start, n), :, pl.ds(pl.multiple_of((bz % 2) * 128, 128), 128)]

    def remote(src, dst, ss, rs, dev):
        return pltpu.make_async_remote_copy(
            src_ref=src, dst_ref=dst, send_sem=ss, recv_sem=rs, device_id=dev, device_id_type=MESH
        )

    mine = pl.ds(pl.multiple_of(c * HC, 128), HC)
    theirs = pl.ds(pl.multiple_of((1 - c) * HC, 128), HC)
    loads = [
        pltpu.make_async_copy(a_hbm, a2.at[0], loc.at[0]),
        pltpu.make_async_copy(t_hbm.at[:, mine], t2.at[0], loc.at[1]),
        pltpu.make_async_copy(r_hbm.at[:, mine], r2.at[0], loc.at[2]),
    ]
    for copy in loads:
        copy.start()

    partners = [sib, device(x, y, z + 1 - 2 * zl, 1 - c)]
    for d in (1, 2, 3):
        partners.append(device((x + d) % 4, y, z, c))
        partners.append(device(x, (y + d) % 4, z, c))
        partners.append(device(x, y, (z + d) % 4, c))
    barrier = pltpu.get_barrier_semaphore()
    for q in partners:
        pl.semaphore_signal(barrier, inc=1, device_id=q, device_id_type=MESH)

    lane = lax.broadcasted_iota(jnp.int32, (1, CAP), 1)
    live = lane < cnt_ref[...].reshape(1, 1)
    weight = jnp.where(live, lw_ref[...], 0).astype(F32)
    magnitude = jnp.sum(jnp.abs(weight), axis=1, keepdims=True)
    rows8 = lax.broadcasted_iota(jnp.int32, (8, CAP), 0)
    meta[0] = jnp.where(
        rows8 == 0,
        jnp.broadcast_to(ref_ref[...], (8, CAP)),
        jnp.where(
            rows8 == 1,
            jnp.broadcast_to(weight, (8, CAP)),
            jnp.where(
                rows8 == 2,
                jnp.broadcast_to(seg_ref[...].astype(F32), (8, CAP)),
                jnp.broadcast_to(magnitude, (8, CAP)),
            ),
        ),
    )

    def shard_columns(core):
        base = core * HC
        return jnp.concatenate(
            [
                w_ref[:, pl.ds(pl.multiple_of(base + zl * 256, 128), 256)].astype(F32),
                w_ref[:, pl.ds(pl.multiple_of(base + 512 + zl * 256, 128), 256)].astype(F32),
                w_ref[:, pl.ds(pl.multiple_of(base + 1024 + zl * 128, 128), 128)].astype(F32),
            ],
            axis=1,
        )

    wx[0] = shard_columns(1 - c)
    gain_row[0, :] = gain_in[...]
    pl.semaphore_wait(barrier, len(partners))

    sib_w = remote(wx.at[0], wx.at[1], sib_s.at[0], sib_r.at[0], sib)
    sib_m = remote(meta.at[0], meta.at[1], sib_s.at[1], sib_r.at[1], sib)
    sib_a = remote(a_hbm, a2.at[1], sib_s.at[2], sib_r.at[2], sib)
    sib_t = remote(t_hbm.at[:, theirs], t2.at[1], sib_s.at[3], sib_r.at[3], sib)
    sib_res = remote(r_hbm.at[:, theirs], r2.at[1], sib_s.at[4], sib_r.at[4], sib)
    for copy in (sib_w, sib_m, sib_a, sib_t, sib_res):
        copy.start()

    own_w = shard_columns(c)
    sib_w.wait_recv()
    got_w = wx[1]
    first = c == 0
    block = jnp.concatenate(
        [jnp.where(first, own_w, got_w), jnp.where(first, got_w, own_w)], axis=0
    ).astype(BF16)
    bx0, by0, bz0 = x, y, z // 2
    wgp[pos(0)[1], pos(0)[0], x] = block[:, 0:256]
    wgn[zl, by0, bz0, bx0] = block[:, 256:512]
    wgn[2, by0, bz0, bx0, :, pl.ds(pl.multiple_of(zl * 128, 128), 128)] = block[:, 512:640]

    ph1, ph2, ph2r, ph3, ph4 = {}, {}, {}, {}, {}
    for p in pieces:
        p1, p2, p3 = pos(p)
        for d in (1, 2, 3):
            slot = wslot(p, p3, p2, p1, 1)
            ph1[p, d] = remote(slot, slot, p1_s.at[p, d - 1], p1_r.at[p, d - 1], peer(p, d, 0, 0))
        line = wslot(p, p3, p2, 0, 4)
        low = wslot(p, p3, (p2 + 3) % 4, 0, 2)
        high = wslot(p, p3, (p2 + 1) % 4, 2, 2)
        ph2[p, 1] = remote(line, line, p2_s.at[p, 0], p2_r.at[p, 0], peer(p, 0, 1, 0))
        ph2[p, 3] = remote(line, line, p2_s.at[p, 1], p2_r.at[p, 1], peer(p, 0, 3, 0))
        ph2r[p, 1] = remote(low, low, p2_s.at[p, 2], p2_r.at[p, 2], peer(p, 0, 1, 0))
        ph2r[p, 3] = remote(high, high, p2_s.at[p, 3], p2_r.at[p, 3], peer(p, 0, 3, 0))
        for d in range(4):
            a2_ = (p2 + d) % 4
            line = wslot(p, p3, a2_, 0, 4)
            low = wslot(p, (p3 + 3) % 4, a2_, 0, 2)
            high = wslot(p, (p3 + 1) % 4, a2_, 2, 2)
            ph3[p, d, 0] = remote(line, line, p3_s.at[p, d, 0], p3_r.at[p, d, 0], peer(p, 0, 0, 1))
            ph3[p, d, 1] = remote(line, line, p3_s.at[p, d, 1], p3_r.at[p, d, 1], peer(p, 0, 0, 3))
            ph4[p, d, 0] = remote(low, low, p4_s.at[p, d, 0], p4_r.at[p, d, 0], peer(p, 0, 0, 1))
            ph4[p, d, 1] = remote(high, high, p4_s.at[p, d, 1], p4_r.at[p, d, 1], peer(p, 0, 0, 3))

    sends = [sib_w, sib_m, sib_a, sib_t, sib_res]

    def start(copy):
        copy.start()
        sends.append(copy)

    def den_phase(axis, value):
        at_ = (x, y, z)[axis]
        den[axis, at_] = value
        copies = []
        for d in (1, 2, 3):
            q = [x, y, z]
            q[axis] = (at_ + d) % 4
            slot = den.at[axis, at_]
            copy = remote(
                slot, slot, den_s.at[axis, d - 1], den_r.at[axis, d - 1], device(q[0], q[1], q[2], c)
            )
            start(copy)
            copies.append(copy)
        return copies

    def den_total(axis, copies):
        for copy in copies:
            copy.wait_recv()
        return den[axis, 0] + den[axis, 1] + den[axis, 2] + den[axis, 3]

    sib_m.wait_recv()
    den_copies = den_phase(0, meta[0, :, 0:128] * 0 + (meta[0, 3:4, 0:128] + meta[1, 3:4, 0:128]))
    for d in (1, 3, 2):
        for p in pieces:
            start(ph1[p, d])

    def transpose_rows(slot):
        @pl.loop(0, DW // 128)
        def _(k):
            off = pl.ds(pl.multiple_of(k * 128, 128), 128)
            at[off, slot * CAP : (slot + 1) * CAP] = a2[slot, :, off].T

    def transpose_targets(slot):
        @pl.loop(0, NG)
        def _(g):
            for k in (0, 1):
                off = pl.ds(pl.multiple_of(g * GW + k * 128, 128), 128)
                tt[g, k * 128 : (k + 1) * 128, slot * CAP : (slot + 1) * CAP] = t2[slot, :, off].T

    def slabs(p, v, h):
        m, n = yz[p]
        rows, weights = [], []
        if p == 0:
            for yy in range(4):
                for zz in range(2):
                    zc = 2 * zz + h
                    rows.append(at[pl.ds(pl.multiple_of(((yy * 2 + zz) * 4 + v) * ROW, 16), ROW), :])
                    weights.append(wgp[zc * m + yy * n, yy * m + zc * n, v])
            side = h
        else:
            side = h * m + (v % 2) * n
            for k in (0, 1):
                by = v * m + (2 * k + h) * n
                bz = k * m + (v // 2) * n
                rows.append(at[pl.ds(pl.multiple_of((by * 2 + bz) * 4 * ROW, 16), 4 * ROW), :])
                if p == 1:
                    weights.append(wgn[side, by, bz].reshape(4 * ROW, GW))
                else:
                    part = wgn[2, by, bz, :, :, pl.ds(pl.multiple_of(side * 128, 128), 128)]
                    weights.append(part.reshape(4 * ROW, 128))
        return jnp.concatenate(rows, axis=0), jnp.concatenate(weights, axis=0), side

    def forward(p, v, only=None):
        @pl.loop(0 if only is None else only, 2 if only is None else only + 1)
        def _(h):
            rows, weights, side = slabs(p, v, h)
            res = lax.dot_general(weights, rows, (((0,), (0,)), ((), ())), preferred_element_type=F32)
            if p == 0:
                pr[side] += res
            elif p == 1:
                pr[2 + side] += res
            else:
                pr[4, pl.ds(pl.multiple_of(side * 128, 128), 128)] += res

    def near(p, d, odd):
        forward(p, last_place(p, d), (pos(p)[1] + odd) % 2)

    def last_place(p, d):
        return (pos(p)[2] + d) % 4

    gcol[...] = jnp.broadcast_to(
        gain_row[:, pl.ds(pl.multiple_of(c * HC, 128), HC)], (128, HC)
    ).T.reshape(NG, GW, 128)

    @pl.loop(0, NG)
    def _(g):
        pr[g] = jnp.zeros((GW, 2 * CAP), F32)

    for copy in loads:
        copy.wait()

    for p in pieces:
        for d in (1, 3, 2):
            ph1[p, d].wait_recv()
        if p == 0:
            den_copies = den_phase(1, den_total(0, den_copies))
        for d in (1, 3):
            start(ph2[p, d])
        if p == 0:
            start(ph3[p, 0, 0])
            start(ph3[p, 0, 1])
    for p in (1, 2):
        start(ph3[p, 0, 0])
        start(ph3[p, 0, 1])

    def spread(p, d):
        if d == 2:
            ph2r[p, 1].wait_recv()
            ph2r[p, 3].wait_recv()
        else:
            ph2[p, 4 - d].wait_recv()
            start(ph2r[p, 4 - d])
        start(ph3[p, d, 0])
        start(ph3[p, d, 1])

    def relay(p, d):
        for s in (0, 1):
            ph3[p, d, s].wait_recv()
            start(ph4[p, d, s])

    spread(0, 1)
    spread(0, 3)
    transpose_rows(0)
    relay(0, 0)
    for d in (1, 3):
        spread(1, d)
        spread(2, d)
    den_copies = den_phase(2, den_total(1, den_copies))
    sib_a.wait_recv()
    transpose_rows(1)
    spread(0, 2)
    relay(0, 1)
    relay(1, 0)
    relay(2, 0)
    forward(0, last_place(0, 0))
    spread(1, 2)
    spread(2, 2)
    sib_t.wait_recv()
    sib_res.wait_recv()
    for slot in (0, 1):
        part = jnp.zeros((CAP, 128), F32)
        for k in range(HC // 128):
            cols = slice(k * 128, (k + 1) * 128)
            part += t2[slot, :, cols].astype(F32) * r2[slot, :, cols].astype(F32)
        sp[0, slot] = jnp.broadcast_to(jnp.sum(part.T, axis=0, keepdims=True), (8, CAP))
    relay(0, 3)
    forward(1, last_place(1, 0))
    relay(1, 1)
    relay(2, 1)
    transpose_targets(0)
    transpose_targets(1)
    forward(2, last_place(2, 0))
    relay(1, 3)
    relay(2, 3)
    near(1, 1, 1)
    near(1, 3, 1)
    relay(0, 2)
    forward(0, last_place(0, 1))
    relay(1, 2)
    relay(2, 2)
    forward(0, last_place(0, 3))
    near(2, 1, 1)
    near(2, 3, 1)
    for p in (1, 2):
        near(p, 1, 0)
        near(p, 3, 0)
    denominator = jnp.maximum(den_total(2, den_copies)[0:1, 0:1], 1.0)
    def arrived(p, steps):
        for d in steps:
            for s in (0, 1):
                ph4[p, d, s].wait_recv()

    arrived(0, ORDER)
    forward(0, last_place(0, 2))
    for odd in (1, 0):
        for p in (1, 2):
            arrived(p, (1, 3) if odd else (0, 2))
            near(p, 2, odd)

    stat[...] = jnp.zeros((2, 8, 2 * CAP), F32)

    @pl.loop(0, NG)
    def _(g):
        for slot in (0, 1):
            cols = slice(slot * CAP, (slot + 1) * CAP)
            gains = jnp.concatenate([gcol[g]] * 4, axis=1)
            p_ = pr[g, :, cols]
            stat[0, :, cols] += jnp.sum((p_ * p_).reshape(GW // 8, 8, CAP), axis=0)
            tp = p_ * tt[g, :, cols].astype(F32) * gains
            stat[1, :, cols] += jnp.sum(tp.reshape(GW // 8, 8, CAP), axis=0)

    row = lax.broadcasted_iota(jnp.int32, (8, CAP), 0)
    for slot in (0, 1):
        cols = slice(slot * CAP, (slot + 1) * CAP)
        q1 = jnp.sum(stat[0, :, cols], axis=0, keepdims=True)
        q3 = jnp.sum(stat[1, :, cols], axis=0, keepdims=True)
        sp[0, slot] = jnp.where(row == 0, q1, jnp.where(row == 1, q3, sp[0, slot]))

    swap = [
        remote(sp.at[0, s], sp.at[1, 1 - s], sib_s.at[5 + s], sib_r.at[5 + s], sib) for s in (0, 1)
    ]
    for copy in swap:
        start(copy)
    for copy in swap:
        copy.wait_recv()

    segs = lax.broadcasted_iota(jnp.int32, (SEGS, CAP), 0).astype(F32)
    for slot in (0, 1):
        total = sp[0, slot] + sp[1, slot]
        q1, q3, q2 = total[0:1], total[1:2], total[2:3]
        scale = jnp.sqrt(q1 * (1.0 / DW) + 1e-06)
        score = q2 + q3 / scale
        ref, wgt, seg = meta[slot, 0:1], meta[slot, 1:2], meta[slot, 2:3]
        forget = jnp.maximum(-wgt, 0.0)
        retain = jnp.maximum(wgt, 0.0)
        table = (seg == segs).astype(F32)
        seg_sum = jnp.sum(table * (forget * (score - ref)), axis=1, keepdims=True)
        has = jnp.sum(table * forget, axis=1, keepdims=True) > 0.5
        scaled = npo_beta * seg_sum
        if slot == 0:
            soft = jnp.maximum(scaled, 0.0) + jnp.log1p(jnp.exp(-jnp.abs(scaled)))
            npo = jnp.sum(jnp.where(has, 2.0 / npo_beta * soft, 0.0), axis=0, keepdims=True)
            loss = npo - jnp.sum(retain * score, axis=1, keepdims=True)
            gsum[0, x, 0:1, HC : HC + 128] = jnp.broadcast_to(loss, (1, 128))
        sig = jnp.sum(table * jax.nn.sigmoid(scaled), axis=0, keepdims=True)
        grad = loss_scale / denominator * (forget * 2.0 * sig - retain)
        alpha[slot] = jnp.broadcast_to(grad / scale, (8, CAP))
        beta[slot] = jnp.broadcast_to(q3 / (scale * scale * DW), (8, CAP))

    @pl.loop(0, NG)
    def _(g):
        gains = jnp.concatenate([gcol[g]] * 4, axis=1)
        part = jnp.zeros((GW, 128), F32)
        for slot in (0, 1):
            cols = slice(slot * CAP, (slot + 1) * CAP)
            al, be = alpha[slot, 0:1], beta[slot, 0:1]
            p_ = pr[g, :, cols]
            t = tt[g, :, cols].astype(F32)
            pg[g, :, cols] = (al * (t * gains - p_ * be)).astype(BF16)
            u = al * t * p_
            part += (u[:, 0:128] + u[:, 128:256]) + (u[:, 256:384] + u[:, 384:512])
        gacc[g] = part

    @pl.loop(0, NG)
    def _(g):
        cols = pl.ds(pl.multiple_of(g * GW, GW), GW)
        gsum[0, x, 0:1, cols] = jnp.sum(gacc[g].T, axis=0, keepdims=True)

    def grad_blocks(p, v, emit):
        m, n = yz[p]
        for h in (0, 1):
            rows, _, side = slabs(p, v, h)
            if p == 2:
                right = pg[4, pl.ds(pl.multiple_of(side * 128, 128), 128)]
            else:
                right = pg[2 * p + side]
            res = lax.dot_general(rows, right, (((1,), (1,)), ((), ())), preferred_element_type=F32)
            for k in range(8):
                value = res[k * ROW : (k + 1) * ROW]
                if p == 0:
                    yy, zc = k // 2, 2 * (k % 2) + h
                    emit(zc * m + yy * n, yy * m + zc * n, value)
                else:
                    emit(2 * (k // 4) + h, k % 4, value)

    q0, qa, q1, q2, q2r, q3 = {}, {}, {}, {}, {}, {}
    for p in pieces:
        p1, p2, p3 = pos(p)
        for s in (0, 1):
            half = pl.ds(2 * s, 2)
            to = peer(p, 0, 0, 1 + 2 * s)
            q0[p, s] = remote(st_o[p].at[:, half], rl[p].at[s], q0_s.at[p, s], q0_r.at[p, s], to)
            free = pl.ds(2 * (1 - s), 2)
            qa[p, s] = remote(
                st_n[p].at[s, :, free], rv[p].at[s, :, free], qa_s.at[p, s], qa_r.at[p, s], to
            )
            for d in range(4):
                i = (p2 + d) % 4
                q1[p, s, d] = remote(
                    st_n[p].at[s, i, half], rv[p].at[s, i, half], q1_s.at[p, s, d], q1_r.at[p, s, d], to
                )
        for t_ in (0, 1):
            to = peer(p, 0, 1 + 2 * t_, 0)
            q2[p, 1 + 2 * t_] = remote(
                s2[p].at[2 * t_], v2[p].at[t_], q2_s.at[p, t_], q2_r.at[p, t_], to
            )
            q2r[p, t_] = remote(
                s2[p].at[1, pl.ds(2 * t_, 2)], w2[p].at[t_], q2_s.at[p, 2 + t_], q2_r.at[p, 2 + t_], to
            )
        for d in (1, 2, 3):
            q3[p, d] = remote(
                s3[p].at[d - 1], v3[p].at[d - 1], q3_s.at[p, d - 1], q3_r.at[p, d - 1], peer(p, d, 0, 0)
            )

    def put(ref, prefix=()):
        def emit(i, j, value):
            ref[prefix + (i, j)] = value.astype(ref.dtype)

        return emit

    def gain_phase(axis):
        at_ = (x, y, z)[axis]
        copies = []
        for d in (1, 2, 3):
            q = [x, y, z]
            q[axis] = (at_ + d) % 4
            slot = gsum.at[axis, at_]
            copy = remote(
                slot, slot, g_s.at[axis, d - 1], g_r.at[axis, d - 1], device(q[0], q[1], q[2], c)
            )
            start(copy)
            copies.append(copy)
        return copies

    def gain_total(axis, copies):
        for copy in copies:
            copy.wait_recv()
        return (gsum[axis, 0] + gsum[axis, 1]) + (gsum[axis, 2] + gsum[axis, 3])

    gain_copies = gain_phase(0)

    for p in (1, 2, 0):
        grad_blocks(p, (pos(p)[2] + 2) % 4, put(st_o[p]))
        start(q0[p, 0])
        start(q0[p, 1])

    for p in (1, 2, 0):
        for t_ in (0, 1):
            grad_blocks(p, (pos(p)[2] + 1 + 2 * t_) % 4, put(st_n[p], (t_,)))
            start(qa[p, t_])

    def relay_sums(p):
        for d in (2, 1, 3, 0):
            i = (pos(p)[1] + d) % 4
            for t_ in (0, 1):
                if d == 2:
                    q0[p, t_].wait_recv()
                half = slice(2 * t_, 2 * t_ + 2)
                both = st_n[p][t_, i, half].astype(F32) + rl[p][t_, i].astype(F32)
                st_n[p][t_, i, half] = both.astype(BF16)
                start(q1[p, t_, d])

    for p in (1, 2):
        grad_blocks(p, pos(p)[2], put(own[p]))
    relay_sums(1)
    relay_sums(2)
    grad_blocks(0, pos(0)[2], put(own[0]))
    relay_sums(0)

    gsum[1, y] = gain_total(0, gain_copies)
    gain_copies = gain_phase(1)

    def lines(h, yy):
        m, n = yz[0]
        out = []
        for zz in range(2):
            zc = 2 * zz + h
            out.append(wgp[zc * m + yy * n, yy * m + zc * n].reshape(4 * ROW, GW))
        return jnp.concatenate(out, axis=0)

    def grad_rows(slot, yy):
        res = jnp.zeros((640, CAP), F32)
        for g in range(NG):
            w = lines(g, yy) if g < 2 else wgn[g - 2, yy].reshape(640, GW)
            right = pg[g, :, slot * CAP : (slot + 1) * CAP]
            res = res + jnp.dot(w, right, preferred_element_type=F32)
        return res

    ga_copies = []

    def sibling_rows(yy):
        rows = slice(yy * 640, (yy + 1) * 640)
        ga_send[rows, :] = grad_rows(1, yy).astype(BF16)
        copy = remote(ga_send.at[rows], ga_recv.at[rows], ga_s.at[yy], ga_r.at[yy], sib)
        start(copy)
        ga_copies.append(copy)

    ga_stores = []

    def own_rows(yy):
        ga_copies[yy].wait_recv()
        rows = slice(yy * 640, (yy + 1) * 640)
        both = (grad_rows(0, yy) + ga_recv[rows, :].astype(F32)).astype(BF16)
        for k in range(5):
            ga_own[:, yy * 640 + k * 128 : yy * 640 + (k + 1) * 128] = both[k * 128 : (k + 1) * 128].T
        copy = pltpu.make_async_copy(ga_own.at[:, rows], ga_out.at[:, rows], loc.at[3 + yy])
        copy.start()
        ga_stores.append(copy)

    def reduce_step(p, d):
        p1, p2, p3 = pos(p)
        i = (p2 + d) % 4
        for t_ in (0, 1):
            if d == 2:
                qa[p, t_].wait_recv()
            q1[p, t_, d].wait_recv()
        total = own[p][i] + rv[p][0, i].astype(F32) + rv[p][1, i].astype(F32)
        if d == 0:
            own[p][i] = total
            return
        s2[p][d - 1] = total.astype(BF16)
        if d == 2:
            start(q2r[p, 0])
            start(q2r[p, 1])
            return
        t_ = d // 2
        half = slice(2 * t_, 2 * t_ + 2)
        q2r[p, t_].wait_recv()
        s2[p][d - 1, half] = (total[half] + w2[p][t_].astype(F32)).astype(BF16)
        start(q2[p, d])

    def second(p):
        p1, p2, p3 = pos(p)
        acc = own[p][p2]
        for t_ in (0, 1):
            q2[p, 1 + 2 * t_].wait_recv()
            acc = acc + v2[p][t_].astype(F32)
        own[p][p2] = acc
        for d in (1, 3, 2):
            s3[p][d - 1] = own[p][p2, (p1 + d) % 4].astype(BF16)
            start(q3[p, d])

    offs = (0, 256, 512)
    zn = z + 1 - 2 * zl
    last = {}

    def third(p):
        p1, p2, p3 = pos(p)
        acc = own[p][p2, p1]
        for d in (1, 3, 2):
            q3[p, d].wait_recv()
            acc = acc + v3[p][d - 1].astype(F32)
        cols = slice(offs[p], offs[p] + WIDTH[p])
        pad = jnp.zeros((PAD - HALF, WIDTH[p]), F32)
        for core in (0, 1):
            part = acc[core * HALF : (core + 1) * HALF]
            fb[core, :, cols] = jnp.concatenate([part, pad], axis=0).astype(BF16)
        mine_ = fb.at[c, :, cols]
        other = fb.at[1 - c, :, cols]
        last[p] = [
            remote(other, fr.at[0, :, cols], qf_s.at[p, 0], qf_r.at[p, 0], sib),
            remote(mine_, fr.at[1, :, cols], qf_s.at[p, 1], qf_r.at[p, 1], device(x, y, zn, c)),
            remote(other, fr.at[2, :, cols], qf_s.at[p, 2], qf_r.at[p, 2], device(x, y, zn, 1 - c)),
        ]
        for copy in (last[p][1], last[p][2], last[p][0]):
            start(copy)

    sibling_rows(0)
    sibling_rows(1)
    sibling_rows(2)
    sibling_rows(3)
    reduce_step(1, 2)
    reduce_step(2, 2)
    own_rows(0)
    own_rows(1)
    reduce_step(0, 2)
    reduce_step(1, 1)
    reduce_step(2, 1)
    reduce_step(1, 3)
    reduce_step(2, 3)
    gsum[2, z] = gain_total(1, gain_copies)
    gain_copies = gain_phase(2)
    reduce_step(0, 1)
    reduce_step(0, 3)
    reduce_step(1, 0)
    reduce_step(2, 0)
    reduce_step(0, 0)
    second(1)
    second(2)
    second(0)
    third(1)
    third(2)

    total = gain_total(2, gain_copies)
    gsib[c] = total
    gcopy = remote(gsib.at[c], gsib.at[c], sib_s.at[8], sib_r.at[8], sib)
    start(gcopy)

    third(0)
    own_rows(2)
    own_rows(3)

    def place_columns(core, side, value):
        base = core * HC
        value = value.astype(F32)[0:HALF]
        gw_out[:, pl.ds(pl.multiple_of(base + side * 256, 128), 256)] = value[:, 0:256]
        gw_out[:, pl.ds(pl.multiple_of(base + 512 + side * 256, 128), 256)] = value[:, 256:512]
        gw_out[:, pl.ds(pl.multiple_of(base + 1024 + side * 128, 128), 128)] = value[:, 512:640]

    place_columns(c, zl, fb[c])

    gcopy.wait_recv()
    gg_out[...] = jnp.concatenate([gsib[0, 0, 0:HC], gsib[1, 0, 0:HC]], axis=0)
    loss_out[...] = (gsib[0, 0:1, HC : HC + 1] + gsib[1, 0:1, HC : HC + 1]) / denominator

    for p in (1, 2, 0):
        for copy in last[p]:
            copy.wait_recv()
    place_columns(1 - c, zl, fr[0])
    place_columns(c, 1 - zl, fr[1])
    place_columns(1 - c, 1 - zl, fr[2])

    for copy in sends:
        copy.wait_send()
    for copy in ga_stores:
        copy.wait()


def scratch():
    dma = pltpu.SemaphoreType.DMA
    vm = pltpu.VMEM
    out = [
        vm((1, DW), F32),
        vm((NG, GW, 128), F32),
        vm((2, CAP, DW), BF16),
        vm((DW, 2 * CAP), BF16),
        vm((2, CAP, HC), BF16),
        vm((2, CAP, HC), BF16),
        vm((NG, GW, 2 * CAP), BF16),
        vm((4, 4, 4, ROW, GW), BF16),
        vm((NG - 2, 4, 2, 4, ROW, GW), BF16),
        vm((NG, GW, 2 * CAP), F32),
        vm((NG, GW, 2 * CAP), BF16),
        vm((2, HALF, 640), F32),
        vm((2, 8, CAP), F32),
        vm((2, 8, 2 * CAP), F32),
        vm((2, 2, 8, CAP), F32),
        vm((2, 8, CAP), F32),
        vm((2, 8, CAP), F32),
        vm((NG, GW, 128), F32),
        vm((3, 4, 8, 128), F32),
        vm((3, 4, 1, HC + 128), F32),
        vm((2, 1, HC + 128), F32),
    ]
    out += [vm((4, 4, ROW, w), BF16) for w in WIDTH]
    out += [vm((2, 4, 4, ROW, w), BF16) for w in WIDTH]
    out += [vm((2, 4, 2, ROW, w), BF16) for w in WIDTH]
    out += [vm((2, 4, 4, ROW, w), BF16) for w in WIDTH]
    out += [vm((4, 4, ROW, w), F32) for w in WIDTH]
    out += [vm((3, 4, ROW, w), BF16) for w in WIDTH]
    out += [vm((2, 4, ROW, w), BF16) for w in WIDTH]
    out += [vm((2, 2, ROW, w), BF16) for w in WIDTH]
    out += [vm((3, ROW, w), BF16) for w in WIDTH]
    out += [vm((3, ROW, w), BF16) for w in WIDTH]
    out += [
        vm((2, PAD, 640), BF16),
        vm((3, PAD, 640), BF16),
        vm((DW, CAP), BF16),
        vm((DW, CAP), BF16),
        vm((CAP, DW), BF16),
        dma((7,)),
    ]
    for shape in (
        (9,), (3, 3), (3, 3), (3, 3), (3, 4), (3, 4, 2), (3, 4, 2),
        (3, 2), (3, 2), (3, 2, 4), (3, 4), (3, 3), (3, 3), (4,),
    ):
        out += [dma(shape), dma(shape)]
    return out


def finish(gw, gg, ga, loss, gw_out, gg_out, ga_out, loss_out, gw_v, gg_v, ga_v, loss_v, s_in, s_out):
    n = CAP // PARTS
    trips = []
    for k in range(PARTS):
        rows = slice(k * n, (k + 1) * n)
        trips.append((ga.at[rows], ga_v.at[rows], ga_out.at[rows]))
    trips += [(gw, gw_v, gw_out), (gg, gg_v, gg_out), (loss, loss_v, loss_out)]
    loads = [pltpu.make_async_copy(src, mid, s_in.at[i]) for i, (src, mid, _) in enumerate(trips)]
    stores = [pltpu.make_async_copy(mid, dst, s_out.at[i]) for i, (_, mid, dst) in enumerate(trips)]
    for copy in loads:
        copy.start()
    for load, store in zip(loads, stores):
        load.wait()
        store.start()
    for copy in stores:
        copy.wait()


def shards(attention_out, residual, target_rows, ref_logit, loss_weight, segment, counts, out_weight, norm_gain):
    any_ = pl.BlockSpec(memory_space=pl.ANY)
    vmem = pl.BlockSpec(memory_space=pltpu.VMEM)
    gw, gg, ga, loss = pl.pallas_call(
        kernel,
        out_shape=(
            jax.ShapeDtypeStruct((HALF, DW), F32),
            jax.ShapeDtypeStruct((DW,), F32),
            jax.ShapeDtypeStruct((CAP, DW), BF16),
            jax.ShapeDtypeStruct((1, 1), F32),
        ),
        in_specs=[any_, any_, any_, vmem, vmem, vmem, vmem, vmem, vmem],
        out_specs=(vmem, vmem, any_, vmem),
        scratch_shapes=scratch(),
        compiler_params=pltpu.CompilerParams(
            collective_id=0, has_side_effects=True, vmem_limit_bytes=62 * 2**20
        ),
        cost_estimate=pl.CostEstimate(
            flops=3 * 2 * CAP * DW * DW, bytes_accessed=4 * CAP * DW * 2, transcendentals=0
        ),
    )(
        attention_out,
        residual,
        target_rows,
        ref_logit,
        loss_weight,
        segment,
        counts,
        out_weight,
        norm_gain,
    )
    gw, gg, ga, loss = pl.pallas_call(
        finish,
        out_shape=(
            jax.ShapeDtypeStruct((HALF, DW), F32),
            jax.ShapeDtypeStruct((DW,), F32),
            jax.ShapeDtypeStruct((CAP, DW), BF16),
            jax.ShapeDtypeStruct((1, 1), F32),
        ),
        in_specs=[any_] * 4,
        out_specs=(any_,) * 4,
        scratch_shapes=[
            pltpu.VMEM((HALF, DW), F32),
            pltpu.VMEM((DW,), F32),
            pltpu.VMEM((CAP, DW), BF16),
            pltpu.VMEM((1, 1), F32),
            pltpu.SemaphoreType.DMA((PARTS + 3,)),
            pltpu.SemaphoreType.DMA((PARTS + 3,)),
        ],
        compiler_params=pltpu.CompilerParams(vmem_limit_bytes=62 * 2**20),
    )(gw, gg, ga, loss)
    return gw, gg, ga, loss[0, 0]


def solution(mesh):
    rows = P(("dp", "fsdp"), None)
    placed = (rows,) * 6 + (P(("dp", "fsdp")), P("fsdp", None), P())
    return jax.shard_map(
        shards,
        mesh=mesh,
        in_specs=placed,
        out_specs=(P("fsdp", None), P(), rows, P()),
        check_vma=False,
    )
```

```python
import functools

import jax
import jax.numpy as jnp
from jax import lax
from jax.experimental import pallas as pl
from jax.experimental.pallas import tpu as pltpu
from jax.sharding import PartitionSpec as P

SEGS = 16
F32 = jnp.float32
BF16 = jnp.bfloat16
MESH = pl.DeviceIdType.MESH

npo_beta = 0.1
loss_scale = 1024.0

ROW = 80
HALF = 40
PAD = 48
CAP = 512
DW = 2560
HC = 1280
GW = 256
NG = HC // GW
WIDTH = (256, 256, 128)
ORDER = (0, 1, 3, 2)
PARTS = 4


def place():
    dp = lax.axis_index("dp")
    f = lax.axis_index("fsdp")
    return (f // 2) % 4, f // 16, ((f // 8) % 2) * 2 + dp, f % 2


def device(x, y, z, c):
    return (z % 2, ((y * 2 + z // 2) * 4 + x) * 2 + c)


def kernel(
    a_hbm,
    r_hbm,
    t_hbm,
    ref_hbm,
    lw_hbm,
    seg_hbm,
    cnt_hbm,
    w_hbm,
    gain_hbm,
    gw_out,
    gg_out,
    ga_out,
    loss_out,
    ref_ref,
    lw_ref,
    seg_ref,
    cnt_ref,
    w_ref,
    gain_in,
    small,
    gain_row,
    gcol,
    a2,
    at,
    t2,
    r2,
    tt,
    wgp,
    wgn,
    pr,
    pg,
    wx,
    meta,
    stat,
    sp,
    alpha,
    beta,
    gacc,
    den,
    gsum,
    gsib,
    st_o0, st_o1, st_o2,
    st_n0, st_n1, st_n2,
    rl0, rl1, rl2,
    rv0, rv1, rv2,
    ow0, ow1, ow2,
    s20, s21, s22,
    v20, v21, v22,
    w20, w21, w22,
    s30, s31, s32,
    v30, v31, v32,
    fb,
    fr,
    ga_send,
    ga_recv,
    ga_own,
    loc,
    sib_s, sib_r,
    den_s, den_r,
    g_s, g_r,
    p1_s, p1_r,
    p2_s, p2_r,
    p3_s, p3_r,
    p4_s, p4_r,
    q0_s, q0_r,
    qa_s, qa_r,
    q1_s, q1_r,
    q2_s, q2_r,
    q3_s, q3_r,
    qf_s, qf_r,
    ga_s, ga_r,
):
    st_o = (st_o0, st_o1, st_o2)
    st_n = (st_n0, st_n1, st_n2)
    rl = (rl0, rl1, rl2)
    rv = (rv0, rv1, rv2)
    own = (ow0, ow1, ow2)
    s2 = (s20, s21, s22)
    v2 = (v20, v21, v22)
    w2 = (w20, w21, w22)
    s3 = (s30, s31, s32)
    v3 = (v30, v31, v32)
    x, y, z, c = place()
    zl = z % 2
    sib = device(x, y, z, 1 - c)
    pieces = range(3)
    yz = ((1 - c, c), (1 - c, c), (c, 1 - c))

    def pos(p):
        m, n = yz[p]
        if p == 0:
            return y * m + z * n, z * m + y * n, x
        return x, z * m + y * n, y * m + z * n

    def coords(p, p1, p2, p3):
        m, n = yz[p]
        if p == 0:
            return p3, p1 * m + p2 * n, p2 * m + p1 * n
        return p1, p3 * m + p2 * n, p2 * m + p3 * n

    def peer(p, d1, d2, d3):
        p1, p2, p3 = pos(p)
        return device(*coords(p, (p1 + d1) % 4, (p2 + d2) % 4, (p3 + d3) % 4), c)

    def wslot(p, a3, a2_, start, n):
        if p == 0:
            return wgp.at[a2_, pl.ds(start, n), a3]
        bx, by, bz = coords(p, 0, a2_, a3)
        if p == 1:
            return wgn.at[bz % 2, by, bz // 2, pl.ds(start, n)]
        return wgn.at[2, by, bz // 2, pl.ds(start, n), :, pl.ds(pl.multiple_of((bz % 2) * 128, 128), 128)]

    def remote(src, dst, ss, rs, dev):
        return pltpu.make_async_remote_copy(
            src_ref=src, dst_ref=dst, send_sem=ss, recv_sem=rs, device_id=dev, device_id_type=MESH
        )

    mine = pl.ds(pl.multiple_of(c * HC, 128), HC)
    theirs = pl.ds(pl.multiple_of((1 - c) * HC, 128), HC)
    inputs = [
        pltpu.make_async_copy(src, dst, small.at[i])
        for i, (src, dst) in enumerate(
            (
                (w_hbm, w_ref),
                (cnt_hbm, cnt_ref),
                (ref_hbm, ref_ref),
                (lw_hbm, lw_ref),
                (seg_hbm, seg_ref),
                (gain_hbm, gain_in),
            )
        )
    ]
    for copy in inputs:
        copy.start()
    loads = [
        pltpu.make_async_copy(a_hbm, a2.at[0], loc.at[0]),
        pltpu.make_async_copy(t_hbm.at[:, mine], t2.at[0], loc.at[1]),
        pltpu.make_async_copy(r_hbm.at[:, mine], r2.at[0], loc.at[2]),
    ]
    for copy in loads:
        copy.start()

    partners = [sib, device(x, y, z + 1 - 2 * zl, 1 - c)]
    for d in (1, 2, 3):
        partners.append(device((x + d) % 4, y, z, c))
        partners.append(device(x, (y + d) % 4, z, c))
        partners.append(device(x, y, (z + d) % 4, c))
    barrier = pltpu.get_barrier_semaphore()
    for q in partners:
        pl.semaphore_signal(barrier, inc=1, device_id=q, device_id_type=MESH)

    for copy in inputs:
        copy.wait()
    lane = lax.broadcasted_iota(jnp.int32, (1, CAP), 1)
    live = lane < cnt_ref[...].reshape(1, 1)
    weight = jnp.where(live, lw_ref[...], 0).astype(F32)
    magnitude = jnp.sum(jnp.abs(weight), axis=1, keepdims=True)
    rows8 = lax.broadcasted_iota(jnp.int32, (8, CAP), 0)
    meta[0] = jnp.where(
        rows8 == 0,
        jnp.broadcast_to(ref_ref[...], (8, CAP)),
        jnp.where(
            rows8 == 1,
            jnp.broadcast_to(weight, (8, CAP)),
            jnp.where(
                rows8 == 2,
                jnp.broadcast_to(seg_ref[...].astype(F32), (8, CAP)),
                jnp.broadcast_to(magnitude, (8, CAP)),
            ),
        ),
    )

    def shard_columns(core):
        base = core * HC
        return jnp.concatenate(
            [
                w_ref[:, pl.ds(pl.multiple_of(base + zl * 256, 128), 256)].astype(F32),
                w_ref[:, pl.ds(pl.multiple_of(base + 512 + zl * 256, 128), 256)].astype(F32),
                w_ref[:, pl.ds(pl.multiple_of(base + 1024 + zl * 128, 128), 128)].astype(F32),
            ],
            axis=1,
        )

    wx[0] = shard_columns(1 - c)
    gain_row[0, :] = gain_in[...]
    pl.semaphore_wait(barrier, len(partners))

    sib_w = remote(wx.at[0], wx.at[1], sib_s.at[0], sib_r.at[0], sib)
    sib_m = remote(meta.at[0], meta.at[1], sib_s.at[1], sib_r.at[1], sib)
    sib_a = remote(a_hbm, a2.at[1], sib_s.at[2], sib_r.at[2], sib)
    sib_t = remote(t_hbm.at[:, theirs], t2.at[1], sib_s.at[3], sib_r.at[3], sib)
    sib_res = remote(r_hbm.at[:, theirs], r2.at[1], sib_s.at[4], sib_r.at[4], sib)
    for copy in (sib_w, sib_m, sib_a, sib_t, sib_res):
        copy.start()

    own_w = shard_columns(c)
    sib_w.wait_recv()
    got_w = wx[1]
    first = c == 0
    block = jnp.concatenate(
        [jnp.where(first, own_w, got_w), jnp.where(first, got_w, own_w)], axis=0
    ).astype(BF16)
    bx0, by0, bz0 = x, y, z // 2
    wgp[pos(0)[1], pos(0)[0], x] = block[:, 0:256]
    wgn[zl, by0, bz0, bx0] = block[:, 256:512]
    wgn[2, by0, bz0, bx0, :, pl.ds(pl.multiple_of(zl * 128, 128), 128)] = block[:, 512:640]

    ph1, ph2, ph2r, ph3, ph4 = {}, {}, {}, {}, {}
    for p in pieces:
        p1, p2, p3 = pos(p)
        for d in (1, 2, 3):
            slot = wslot(p, p3, p2, p1, 1)
            ph1[p, d] = remote(slot, slot, p1_s.at[p, d - 1], p1_r.at[p, d - 1], peer(p, d, 0, 0))
        line = wslot(p, p3, p2, 0, 4)
        low = wslot(p, p3, (p2 + 3) % 4, 0, 2)
        high = wslot(p, p3, (p2 + 1) % 4, 2, 2)
        ph2[p, 1] = remote(line, line, p2_s.at[p, 0], p2_r.at[p, 0], peer(p, 0, 1, 0))
        ph2[p, 3] = remote(line, line, p2_s.at[p, 1], p2_r.at[p, 1], peer(p, 0, 3, 0))
        ph2r[p, 1] = remote(low, low, p2_s.at[p, 2], p2_r.at[p, 2], peer(p, 0, 1, 0))
        ph2r[p, 3] = remote(high, high, p2_s.at[p, 3], p2_r.at[p, 3], peer(p, 0, 3, 0))
        for d in range(4):
            a2_ = (p2 + d) % 4
            line = wslot(p, p3, a2_, 0, 4)
            low = wslot(p, (p3 + 3) % 4, a2_, 0, 2)
            high = wslot(p, (p3 + 1) % 4, a2_, 2, 2)
            ph3[p, d, 0] = remote(line, line, p3_s.at[p, d, 0], p3_r.at[p, d, 0], peer(p, 0, 0, 1))
            ph3[p, d, 1] = remote(line, line, p3_s.at[p, d, 1], p3_r.at[p, d, 1], peer(p, 0, 0, 3))
            ph4[p, d, 0] = remote(low, low, p4_s.at[p, d, 0], p4_r.at[p, d, 0], peer(p, 0, 0, 1))
            ph4[p, d, 1] = remote(high, high, p4_s.at[p, d, 1], p4_r.at[p, d, 1], peer(p, 0, 0, 3))

    sends = [sib_w, sib_m, sib_a, sib_t, sib_res]

    def start(copy):
        copy.start()
        sends.append(copy)

    def den_phase(axis, value):
        at_ = (x, y, z)[axis]
        den[axis, at_] = value
        copies = []
        for d in (1, 2, 3):
            q = [x, y, z]
            q[axis] = (at_ + d) % 4
            slot = den.at[axis, at_]
            copy = remote(
                slot, slot, den_s.at[axis, d - 1], den_r.at[axis, d - 1], device(q[0], q[1], q[2], c)
            )
            start(copy)
            copies.append(copy)
        return copies

    def den_total(axis, copies):
        for copy in copies:
            copy.wait_recv()
        return den[axis, 0] + den[axis, 1] + den[axis, 2] + den[axis, 3]

    sib_m.wait_recv()
    den_copies = den_phase(0, meta[0, :, 0:128] * 0 + (meta[0, 3:4, 0:128] + meta[1, 3:4, 0:128]))
    for d in (1, 3, 2):
        for p in pieces:
            start(ph1[p, d])

    def transpose_rows(slot):
        @pl.loop(0, DW // 128)
        def _(k):
            off = pl.ds(pl.multiple_of(k * 128, 128), 128)
            at[off, slot * CAP : (slot + 1) * CAP] = a2[slot, :, off].T

    def transpose_targets(slot):
        @pl.loop(0, NG)
        def _(g):
            for k in (0, 1):
                off = pl.ds(pl.multiple_of(g * GW + k * 128, 128), 128)
                tt[g, k * 128 : (k + 1) * 128, slot * CAP : (slot + 1) * CAP] = t2[slot, :, off].T

    def slabs(p, v, h):
        m, n = yz[p]
        rows, weights = [], []
        if p == 0:
            for yy in range(4):
                for zz in range(2):
                    zc = 2 * zz + h
                    rows.append(at[pl.ds(pl.multiple_of(((yy * 2 + zz) * 4 + v) * ROW, 16), ROW), :])
                    weights.append(wgp[zc * m + yy * n, yy * m + zc * n, v])
            side = h
        else:
            side = h * m + (v % 2) * n
            for k in (0, 1):
                by = v * m + (2 * k + h) * n
                bz = k * m + (v // 2) * n
                rows.append(at[pl.ds(pl.multiple_of((by * 2 + bz) * 4 * ROW, 16), 4 * ROW), :])
                if p == 1:
                    weights.append(wgn[side, by, bz].reshape(4 * ROW, GW))
                else:
                    part = wgn[2, by, bz, :, :, pl.ds(pl.multiple_of(side * 128, 128), 128)]
                    weights.append(part.reshape(4 * ROW, 128))
        return jnp.concatenate(rows, axis=0), jnp.concatenate(weights, axis=0), side

    def forward(p, v, only=None):
        @pl.loop(0 if only is None else only, 2 if only is None else only + 1)
        def _(h):
            rows, weights, side = slabs(p, v, h)
            res = lax.dot_general(weights, rows, (((0,), (0,)), ((), ())), preferred_element_type=F32)
            if p == 0:
                pr[side] += res
            elif p == 1:
                pr[2 + side] += res
            else:
                pr[4, pl.ds(pl.multiple_of(side * 128, 128), 128)] += res

    def near(p, d, odd):
        forward(p, last_place(p, d), (pos(p)[1] + odd) % 2)

    def last_place(p, d):
        return (pos(p)[2] + d) % 4

    gcol[...] = jnp.broadcast_to(
        gain_row[:, pl.ds(pl.multiple_of(c * HC, 128), HC)], (128, HC)
    ).T.reshape(NG, GW, 128)

    @pl.loop(0, NG)
    def _(g):
        pr[g] = jnp.zeros((GW, 2 * CAP), F32)

    for copy in loads:
        copy.wait()

    den_copies = [den_copies]

    def spread_own(p):
        for d in (1, 3, 2):
            ph1[p, d].wait_recv()
        if p == 0:
            den_copies.append(den_phase(1, den_total(0, den_copies[0])))
        for d in (1, 3):
            start(ph2[p, d])

    def spread(p, d):
        if d == 2:
            ph2r[p, 1].wait_recv()
            ph2r[p, 3].wait_recv()
        else:
            ph2[p, 4 - d].wait_recv()
            start(ph2r[p, 4 - d])
        start(ph3[p, d, 0])
        start(ph3[p, d, 1])

    def relay(p, d):
        for s in (0, 1):
            ph3[p, d, s].wait_recv()
            start(ph4[p, d, s])

    def arrived(p, steps):
        for d in steps:
            for s in (0, 1):
                ph4[p, d, s].wait_recv()

    transpose_rows(0)
    spread_own(0)
    start(ph3[0, 0, 0])
    start(ph3[0, 0, 1])
    spread_own(1)
    spread_own(2)
    start(ph3[2, 0, 0])
    start(ph3[2, 0, 1])
    sib_a.wait_recv()
    transpose_rows(1)
    spread(0, 3)
    spread(0, 1)
    spread(2, 3)
    sib_t.wait_recv()
    transpose_targets(0)
    transpose_targets(1)
    spread(2, 1)
    sib_res.wait_recv()
    for slot in (0, 1):
        part = jnp.zeros((CAP, 128), F32)
        for k in range(HC // 128):
            cols = slice(k * 128, (k + 1) * 128)
            part += t2[slot, :, cols].astype(F32) * r2[slot, :, cols].astype(F32)
        sp[0, slot] = jnp.broadcast_to(jnp.sum(part.T, axis=0, keepdims=True), (8, CAP))
    spread(1, 1)
    spread(0, 2)
    relay(2, 1)
    relay(2, 0)
    relay(2, 3)
    spread(2, 2)
    spread(1, 3)
    den_copies = den_phase(2, den_total(1, den_copies[1]))
    relay(0, 3)
    forward(2, last_place(2, 0))
    forward(0, last_place(0, 0))
    relay(0, 1)
    near(2, 3, 1)
    spread(1, 2)
    relay(2, 2)
    forward(1, last_place(1, 0))
    relay(0, 2)
    relay(0, 0)
    arrived(2, (1, 3))
    near(2, 2, 1)
    near(2, 1, 1)
    start(ph3[1, 0, 0])
    start(ph3[1, 0, 1])
    forward(0, last_place(0, 1))
    relay(1, 1)
    relay(1, 3)
    near(2, 3, 0)
    arrived(2, (0, 2))
    near(2, 2, 0)
    near(2, 1, 0)
    relay(1, 2)
    forward(0, last_place(0, 3))
    near(1, 3, 1)
    relay(1, 0)
    near(1, 1, 1)
    near(1, 3, 0)
    near(1, 1, 0)
    arrived(1, (1, 3))
    near(1, 2, 1)
    arrived(0, ORDER)
    forward(0, last_place(0, 2))
    arrived(1, (0, 2))
    near(1, 2, 0)
    denominator = jnp.maximum(den_total(2, den_copies)[0:1, 0:1], 1.0)
    stat[...] = jnp.zeros((2, 8, 2 * CAP), F32)

    @pl.loop(0, NG)
    def _(g):
        for slot in (0, 1):
            cols = slice(slot * CAP, (slot + 1) * CAP)
            gains = jnp.concatenate([gcol[g]] * 4, axis=1)
            p_ = pr[g, :, cols]
            stat[0, :, cols] += jnp.sum((p_ * p_).reshape(GW // 8, 8, CAP), axis=0)
            tp = p_ * tt[g, :, cols].astype(F32) * gains
            stat[1, :, cols] += jnp.sum(tp.reshape(GW // 8, 8, CAP), axis=0)

    row = lax.broadcasted_iota(jnp.int32, (8, CAP), 0)
    for slot in (0, 1):
        cols = slice(slot * CAP, (slot + 1) * CAP)
        q1 = jnp.sum(stat[0, :, cols], axis=0, keepdims=True)
        q3 = jnp.sum(stat[1, :, cols], axis=0, keepdims=True)
        sp[0, slot] = jnp.where(row == 0, q1, jnp.where(row == 1, q3, sp[0, slot]))

    swap = [
        remote(sp.at[0, s], sp.at[1, 1 - s], sib_s.at[5 + s], sib_r.at[5 + s], sib) for s in (0, 1)
    ]
    for copy in swap:
        start(copy)
    for copy in swap:
        copy.wait_recv()

    segs = lax.broadcasted_iota(jnp.int32, (SEGS, CAP), 0).astype(F32)
    for slot in (0, 1):
        total = sp[0, slot] + sp[1, slot]
        q1, q3, q2 = total[0:1], total[1:2], total[2:3]
        scale = jnp.sqrt(q1 * (1.0 / DW) + 1e-06)
        score = q2 + q3 / scale
        ref, wgt, seg = meta[slot, 0:1], meta[slot, 1:2], meta[slot, 2:3]
        forget = jnp.maximum(-wgt, 0.0)
        retain = jnp.maximum(wgt, 0.0)
        table = (seg == segs).astype(F32)
        seg_sum = jnp.sum(table * (forget * (score - ref)), axis=1, keepdims=True)
        has = jnp.sum(table * forget, axis=1, keepdims=True) > 0.5
        scaled = npo_beta * seg_sum
        if slot == 0:
            soft = jnp.maximum(scaled, 0.0) + jnp.log1p(jnp.exp(-jnp.abs(scaled)))
            npo = jnp.sum(jnp.where(has, 2.0 / npo_beta * soft, 0.0), axis=0, keepdims=True)
            loss = npo - jnp.sum(retain * score, axis=1, keepdims=True)
            gsum[0, x, 0:1, HC : HC + 128] = jnp.broadcast_to(loss, (1, 128))
        sig = jnp.sum(table * jax.nn.sigmoid(scaled), axis=0, keepdims=True)
        grad = loss_scale / denominator * (forget * 2.0 * sig - retain)
        alpha[slot] = jnp.broadcast_to(grad / scale, (8, CAP))
        beta[slot] = jnp.broadcast_to(q3 / (scale * scale * DW), (8, CAP))

    @pl.loop(0, NG)
    def _(g):
        gains = jnp.concatenate([gcol[g]] * 4, axis=1)
        part = jnp.zeros((GW, 128), F32)
        for slot in (0, 1):
            cols = slice(slot * CAP, (slot + 1) * CAP)
            al, be = alpha[slot, 0:1], beta[slot, 0:1]
            p_ = pr[g, :, cols]
            t = tt[g, :, cols].astype(F32)
            pg[g, :, cols] = (al * (t * gains - p_ * be)).astype(BF16)
            u = al * t * p_
            part += (u[:, 0:128] + u[:, 128:256]) + (u[:, 256:384] + u[:, 384:512])
        gacc[g] = part

    @pl.loop(0, NG)
    def _(g):
        cols = pl.ds(pl.multiple_of(g * GW, GW), GW)
        gsum[0, x, 0:1, cols] = jnp.sum(gacc[g].T, axis=0, keepdims=True)

    def grad_blocks(p, v, emit):
        m, n = yz[p]
        for h in (0, 1):
            rows, _, side = slabs(p, v, h)
            if p == 2:
                right = pg[4, pl.ds(pl.multiple_of(side * 128, 128), 128)]
            else:
                right = pg[2 * p + side]
            res = lax.dot_general(rows, right, (((1,), (1,)), ((), ())), preferred_element_type=F32)
            for k in range(8):
                value = res[k * ROW : (k + 1) * ROW]
                if p == 0:
                    yy, zc = k // 2, 2 * (k % 2) + h
                    emit(zc * m + yy * n, yy * m + zc * n, value)
                else:
                    emit(2 * (k // 4) + h, k % 4, value)

    q0, qa, q1, q2, q2r, q3 = {}, {}, {}, {}, {}, {}
    for p in pieces:
        p1, p2, p3 = pos(p)
        for s in (0, 1):
            half = pl.ds(2 * s, 2)
            to = peer(p, 0, 0, 1 + 2 * s)
            q0[p, s] = remote(st_o[p].at[:, half], rl[p].at[s], q0_s.at[p, s], q0_r.at[p, s], to)
            free = pl.ds(2 * (1 - s), 2)
            for d in range(4):
                i = (p2 + d) % 4
                qa[p, s, d] = remote(
                    st_n[p].at[s, i, free], rv[p].at[s, i, free], qa_s.at[p, s, d], qa_r.at[p, s, d], to
                )
                q1[p, s, d] = remote(
                    st_n[p].at[s, i, half], rv[p].at[s, i, half], q1_s.at[p, s, d], q1_r.at[p, s, d], to
                )
        for t_ in (0, 1):
            to = peer(p, 0, 1 + 2 * t_, 0)
            q2[p, 1 + 2 * t_] = remote(
                s2[p].at[2 * t_], v2[p].at[t_], q2_s.at[p, t_], q2_r.at[p, t_], to
            )
            q2r[p, t_] = remote(
                s2[p].at[1, pl.ds(2 * t_, 2)], w2[p].at[t_], q2_s.at[p, 2 + t_], q2_r.at[p, 2 + t_], to
            )
        for d in (1, 2, 3):
            q3[p, d] = remote(
                s3[p].at[d - 1], v3[p].at[d - 1], q3_s.at[p, d - 1], q3_r.at[p, d - 1], peer(p, d, 0, 0)
            )

    def put(ref, prefix=()):
        def emit(i, j, value):
            ref[prefix + (i, j)] = value.astype(ref.dtype)

        return emit

    def gain_phase(axis):
        at_ = (x, y, z)[axis]
        copies = []
        for d in (1, 2, 3):
            q = [x, y, z]
            q[axis] = (at_ + d) % 4
            slot = gsum.at[axis, at_]
            copy = remote(
                slot, slot, g_s.at[axis, d - 1], g_r.at[axis, d - 1], device(q[0], q[1], q[2], c)
            )
            start(copy)
            copies.append(copy)
        return copies

    def gain_total(axis, copies):
        for copy in copies:
            copy.wait_recv()
        return (gsum[axis, 0] + gsum[axis, 1]) + (gsum[axis, 2] + gsum[axis, 3])

    waited = set()

    def await_once(name, copy):
        if name not in waited:
            waited.add(name)
            copy.wait_recv()

    def first_blocks(p):
        grad_blocks(p, (pos(p)[2] + 2) % 4, put(st_o[p]))
        start(q0[p, 0])
        start(q0[p, 1])

    def near_blocks(p, t_):
        grad_blocks(p, (pos(p)[2] + 1 + 2 * t_) % 4, put(st_n[p], (t_,)))
        start(qa[p, t_, 2])
        start(qa[p, t_, 1])

    def relay_sum(p, d):
        i = (pos(p)[1] + d) % 4
        for t_ in (0, 1):
            await_once(("q0", p, t_), q0[p, t_])
            half = slice(2 * t_, 2 * t_ + 2)
            both = st_n[p][t_, i, half].astype(F32) + rl[p][t_, i].astype(F32)
            st_n[p][t_, i, half] = both.astype(BF16)
            start(q1[p, t_, d])
            if d in (1, 3):
                start(qa[p, t_, 3 if d == 1 else 0])

    def lines(h, yy):
        m, n = yz[0]
        out = []
        for zz in range(2):
            zc = 2 * zz + h
            out.append(wgp[zc * m + yy * n, yy * m + zc * n].reshape(4 * ROW, GW))
        return jnp.concatenate(out, axis=0)

    def grad_rows(slot, yy):
        res = jnp.zeros((640, CAP), F32)
        for g in range(NG):
            w = lines(g, yy) if g < 2 else wgn[g - 2, yy].reshape(640, GW)
            right = pg[g, :, slot * CAP : (slot + 1) * CAP]
            res = res + jnp.dot(w, right, preferred_element_type=F32)
        return res

    ga_copies = {}

    def sibling_rows(yy):
        rows = slice(yy * 640, (yy + 1) * 640)
        ga_send[rows, :] = grad_rows(1, yy).astype(BF16)
        copy = remote(ga_send.at[rows], ga_recv.at[rows], ga_s.at[yy], ga_r.at[yy], sib)
        start(copy)
        ga_copies[yy] = copy

    ga_stores = []

    def own_rows(yy):
        ga_copies[yy].wait_recv()
        rows = slice(yy * 640, (yy + 1) * 640)
        both = (grad_rows(0, yy) + ga_recv[rows, :].astype(F32)).astype(BF16)
        for k in range(5):
            ga_own[:, yy * 640 + k * 128 : yy * 640 + (k + 1) * 128] = both[k * 128 : (k + 1) * 128].T
        copy = pltpu.make_async_copy(ga_own.at[:, rows], ga_out.at[:, rows], loc.at[3 + yy])
        copy.start()
        ga_stores.append(copy)

    def reduce_step(p, d):
        p1, p2, p3 = pos(p)
        i = (p2 + d) % 4
        for t_ in (0, 1):
            qa[p, t_, d].wait_recv()
            q1[p, t_, d].wait_recv()
        total = own[p][i] + rv[p][0, i].astype(F32) + rv[p][1, i].astype(F32)
        if d == 0:
            own[p][i] = total
            return
        s2[p][d - 1] = total.astype(BF16)
        if d == 2:
            start(q2r[p, 0])
            start(q2r[p, 1])
            return
        t_ = d // 2
        half = slice(2 * t_, 2 * t_ + 2)
        q2r[p, t_].wait_recv()
        s2[p][d - 1, half] = (total[half] + w2[p][t_].astype(F32)).astype(BF16)
        start(q2[p, d])

    def second(p):
        p1, p2, p3 = pos(p)
        acc = own[p][p2]
        for t_ in (0, 1):
            q2[p, 1 + 2 * t_].wait_recv()
            acc = acc + v2[p][t_].astype(F32)
        own[p][p2] = acc
        for d in (1, 3, 2):
            s3[p][d - 1] = own[p][p2, (p1 + d) % 4].astype(BF16)
            start(q3[p, d])

    offs = (0, 256, 512)
    zn = z + 1 - 2 * zl
    last = {}

    def third(p):
        p1, p2, p3 = pos(p)
        acc = own[p][p2, p1]
        for d in (1, 3, 2):
            q3[p, d].wait_recv()
            acc = acc + v3[p][d - 1].astype(F32)
        cols = slice(offs[p], offs[p] + WIDTH[p])
        pad = jnp.zeros((PAD - HALF, WIDTH[p]), F32)
        for core in (0, 1):
            part = acc[core * HALF : (core + 1) * HALF]
            fb[core, :, cols] = jnp.concatenate([part, pad], axis=0).astype(BF16)
        mine_ = fb.at[c, :, cols]
        other = fb.at[1 - c, :, cols]
        last[p] = [
            remote(other, fr.at[0, :, cols], qf_s.at[p, 0], qf_r.at[p, 0], sib),
            remote(mine_, fr.at[1, :, cols], qf_s.at[p, 1], qf_r.at[p, 1], device(x, y, zn, c)),
            remote(other, fr.at[2, :, cols], qf_s.at[p, 2], qf_r.at[p, 2], device(x, y, zn, 1 - c)),
        ]
        for copy in (last[p][1], last[p][2], last[p][0]):
            start(copy)

    gain_copies = gain_phase(0)
    first_blocks(1)
    first_blocks(0)
    first_blocks(2)
    near_blocks(0, 1)
    near_blocks(1, 0)
    near_blocks(2, 0)
    near_blocks(1, 1)
    near_blocks(2, 1)
    grad_blocks(2, pos(2)[2], put(own[2]))
    relay_sum(1, 2)
    relay_sum(2, 2)
    near_blocks(0, 0)
    relay_sum(2, 1)
    relay_sum(0, 2)
    relay_sum(1, 1)
    sibling_rows(0)
    reduce_step(2, 2)
    grad_blocks(1, pos(1)[2], put(own[1]))
    relay_sum(1, 3)
    reduce_step(1, 2)
    relay_sum(0, 1)
    relay_sum(2, 3)
    grad_blocks(0, pos(0)[2], put(own[0]))
    relay_sum(1, 0)
    sibling_rows(3)
    sibling_rows(2)
    sibling_rows(1)
    relay_sum(0, 3)
    relay_sum(2, 0)
    reduce_step(0, 2)
    reduce_step(1, 1)
    gsum[1, y] = gain_total(0, gain_copies)
    gain_copies = gain_phase(1)
    reduce_step(1, 3)
    own_rows(0)
    reduce_step(1, 0)
    reduce_step(2, 1)
    reduce_step(2, 3)
    relay_sum(0, 0)
    reduce_step(0, 1)
    reduce_step(0, 3)
    second(1)
    gsum[2, z] = gain_total(1, gain_copies)
    gain_copies = gain_phase(2)
    own_rows(2)
    reduce_step(2, 0)
    second(2)
    reduce_step(0, 0)
    second(0)
    third(1)
    third(2)
    total = gain_total(2, gain_copies)
    gsib[c] = total
    gcopy = remote(gsib.at[c], gsib.at[c], sib_s.at[8], sib_r.at[8], sib)
    start(gcopy)
    third(0)
    own_rows(3)
    own_rows(1)

    def place_columns(core, side, value):
        base = core * HC
        value = value.astype(F32)[0:HALF]
        gw_out[:, pl.ds(pl.multiple_of(base + side * 256, 128), 256)] = value[:, 0:256]
        gw_out[:, pl.ds(pl.multiple_of(base + 512 + side * 256, 128), 256)] = value[:, 256:512]
        gw_out[:, pl.ds(pl.multiple_of(base + 1024 + side * 128, 128), 128)] = value[:, 512:640]

    place_columns(c, zl, fb[c])

    gcopy.wait_recv()
    gg_out[...] = jnp.concatenate([gsib[0, 0, 0:HC], gsib[1, 0, 0:HC]], axis=0)
    loss_out[...] = (gsib[0, 0:1, HC : HC + 1] + gsib[1, 0:1, HC : HC + 1]) / denominator

    for p in (1, 2, 0):
        for copy in last[p]:
            copy.wait_recv()
    place_columns(1 - c, zl, fr[0])
    place_columns(c, 1 - zl, fr[1])
    place_columns(1 - c, 1 - zl, fr[2])

    for copy in sends:
        copy.wait_send()
    for copy in ga_stores:
        copy.wait()


def scratch():
    dma = pltpu.SemaphoreType.DMA
    vm = pltpu.VMEM
    out = [
        vm((1, CAP), F32),
        vm((1, CAP), jnp.int32),
        vm((1, CAP), jnp.int32),
        vm((1,), jnp.int32),
        vm((HALF, DW), BF16),
        vm((DW,), F32),
        dma((6,)),
        vm((1, DW), F32),
        vm((NG, GW, 128), F32),
        vm((2, CAP, DW), BF16),
        vm((DW, 2 * CAP), BF16),
        vm((2, CAP, HC), BF16),
        vm((2, CAP, HC), BF16),
        vm((NG, GW, 2 * CAP), BF16),
        vm((4, 4, 4, ROW, GW), BF16),
        vm((NG - 2, 4, 2, 4, ROW, GW), BF16),
        vm((NG, GW, 2 * CAP), F32),
        vm((NG, GW, 2 * CAP), BF16),
        vm((2, HALF, 640), F32),
        vm((2, 8, CAP), F32),
        vm((2, 8, 2 * CAP), F32),
        vm((2, 2, 8, CAP), F32),
        vm((2, 8, CAP), F32),
        vm((2, 8, CAP), F32),
        vm((NG, GW, 128), F32),
        vm((3, 4, 8, 128), F32),
        vm((3, 4, 1, HC + 128), F32),
        vm((2, 1, HC + 128), F32),
    ]
    out += [vm((4, 4, ROW, w), BF16) for w in WIDTH]
    out += [vm((2, 4, 4, ROW, w), BF16) for w in WIDTH]
    out += [vm((2, 4, 2, ROW, w), BF16) for w in WIDTH]
    out += [vm((2, 4, 4, ROW, w), BF16) for w in WIDTH]
    out += [vm((4, 4, ROW, w), F32) for w in WIDTH]
    out += [vm((3, 4, ROW, w), BF16) for w in WIDTH]
    out += [vm((2, 4, ROW, w), BF16) for w in WIDTH]
    out += [vm((2, 2, ROW, w), BF16) for w in WIDTH]
    out += [vm((3, ROW, w), BF16) for w in WIDTH]
    out += [vm((3, ROW, w), BF16) for w in WIDTH]
    out += [
        vm((2, PAD, 640), BF16),
        vm((3, PAD, 640), BF16),
        vm((DW, CAP), BF16),
        vm((DW, CAP), BF16),
        vm((CAP, DW), BF16),
        dma((7,)),
    ]
    for shape in (
        (9,), (3, 3), (3, 3), (3, 3), (3, 4), (3, 4, 2), (3, 4, 2),
        (3, 2), (3, 2, 4), (3, 2, 4), (3, 4), (3, 3), (3, 3), (4,),
    ):
        out += [dma(shape), dma(shape)]
    return out


def finish(gw, gg, ga, loss, gw_out, gg_out, ga_out, loss_out, gw_v, gg_v, ga_v, loss_v, s_in, s_out):
    n = CAP // PARTS
    trips = []
    for k in range(PARTS):
        rows = slice(k * n, (k + 1) * n)
        trips.append((ga.at[rows], ga_v.at[rows], ga_out.at[rows]))
    trips += [(gw, gw_v, gw_out), (gg, gg_v, gg_out), (loss, loss_v, loss_out)]
    loads = [pltpu.make_async_copy(src, mid, s_in.at[i]) for i, (src, mid, _) in enumerate(trips)]
    stores = [pltpu.make_async_copy(mid, dst, s_out.at[i]) for i, (_, mid, dst) in enumerate(trips)]
    for copy in loads:
        copy.start()
    for load, store in zip(loads, stores):
        load.wait()
        store.start()
    for copy in stores:
        copy.wait()


def shards(attention_out, residual, target_rows, ref_logit, loss_weight, segment, counts, out_weight, norm_gain):
    any_ = pl.BlockSpec(memory_space=pl.ANY)
    vmem = pl.BlockSpec(memory_space=pltpu.VMEM)
    gw, gg, ga, loss = pl.pallas_call(
        kernel,
        out_shape=(
            jax.ShapeDtypeStruct((HALF, DW), F32),
            jax.ShapeDtypeStruct((DW,), F32),
            jax.ShapeDtypeStruct((CAP, DW), BF16),
            jax.ShapeDtypeStruct((1, 1), F32),
        ),
        in_specs=[any_] * 9,
        out_specs=(vmem, vmem, any_, vmem),
        scratch_shapes=scratch(),
        compiler_params=pltpu.CompilerParams(
            collective_id=0, has_side_effects=True, vmem_limit_bytes=62 * 2**20
        ),
        cost_estimate=pl.CostEstimate(
            flops=3 * 2 * CAP * DW * DW, bytes_accessed=4 * CAP * DW * 2, transcendentals=0
        ),
    )(
        attention_out,
        residual,
        target_rows,
        ref_logit,
        loss_weight,
        segment,
        counts,
        out_weight,
        norm_gain,
    )
    gw, gg, ga, loss = pl.pallas_call(
        finish,
        out_shape=(
            jax.ShapeDtypeStruct((HALF, DW), F32),
            jax.ShapeDtypeStruct((DW,), F32),
            jax.ShapeDtypeStruct((CAP, DW), BF16),
            jax.ShapeDtypeStruct((1, 1), F32),
        ),
        in_specs=[any_] * 4,
        out_specs=(any_,) * 4,
        scratch_shapes=[
            pltpu.VMEM((HALF, DW), F32),
            pltpu.VMEM((DW,), F32),
            pltpu.VMEM((CAP, DW), BF16),
            pltpu.VMEM((1, 1), F32),
            pltpu.SemaphoreType.DMA((PARTS + 3,)),
            pltpu.SemaphoreType.DMA((PARTS + 3,)),
        ],
        compiler_params=pltpu.CompilerParams(vmem_limit_bytes=62 * 2**20),
    )(gw, gg, ga, loss)
    return gw, gg, ga, loss[0, 0]


def solution(mesh):
    rows = P(("dp", "fsdp"), None)
    placed = (rows,) * 6 + (P(("dp", "fsdp")), P("fsdp", None), P())
    return jax.shard_map(
        shards,
        mesh=mesh,
        in_specs=placed,
        out_specs=(P("fsdp", None), P(), rows, P()),
        check_vma=False,
    )
```

```python
import functools

import jax
import jax.numpy as jnp
from jax import lax
from jax.experimental import pallas as pl
from jax.experimental.pallas import tpu as pltpu
from jax.sharding import PartitionSpec as P

SEGS = 16
F32 = jnp.float32
BF16 = jnp.bfloat16
MESH = pl.DeviceIdType.MESH

npo_beta = 0.1
loss_scale = 1024.0

ROW = 80
HALF = 40
PAD = 48
CAP = 512
DW = 2560
HC = 1280
GW = 256
NG = HC // GW
WIDTH = (256, 256, 128)
ORDER = (0, 1, 3, 2)
PARTS = 4


def place():
    dp = lax.axis_index("dp")
    f = lax.axis_index("fsdp")
    return (f // 2) % 4, f // 16, ((f // 8) % 2) * 2 + dp, f % 2


def device(x, y, z, c):
    return (z % 2, ((y * 2 + z // 2) * 4 + x) * 2 + c)


def kernel(
    a_hbm,
    r_hbm,
    t_hbm,
    ref_hbm,
    lw_hbm,
    seg_hbm,
    cnt_hbm,
    w_hbm,
    gain_hbm,
    gw_out,
    gg_out,
    ga_out,
    loss_out,
    ref_ref,
    lw_ref,
    seg_ref,
    cnt_ref,
    w_ref,
    gain_in,
    small,
    gain_row,
    gcol,
    a2,
    at,
    t2,
    r2,
    tt,
    wgp,
    wgn,
    pr,
    pg,
    wx,
    meta,
    stat,
    sp,
    alpha,
    beta,
    gacc,
    den,
    gsum,
    gsib,
    st_o0, st_o1, st_o2,
    st_n0, st_n1, st_n2,
    rl0, rl1, rl2,
    rv0, rv1, rv2,
    ow0, ow1, ow2,
    s20, s21, s22,
    v20, v21, v22,
    w20, w21, w22,
    s30, s31, s32,
    v30, v31, v32,
    fb,
    fr,
    ga_send,
    ga_recv,
    ga_own,
    loc,
    sib_s, sib_r,
    den_s, den_r,
    g_s, g_r,
    p1_s, p1_r,
    p2_s, p2_r,
    p3_s, p3_r,
    p4_s, p4_r,
    q0_s, q0_r,
    qa_s, qa_r,
    q1_s, q1_r,
    q2_s, q2_r,
    q3_s, q3_r,
    qf_s, qf_r,
    ga_s, ga_r,
):
    st_o = (st_o0, st_o1, st_o2)
    st_n = (st_n0, st_n1, st_n2)
    rl = (rl0, rl1, rl2)
    rv = (rv0, rv1, rv2)
    own = (ow0, ow1, ow2)
    s2 = (s20, s21, s22)
    v2 = (v20, v21, v22)
    w2 = (w20, w21, w22)
    s3 = (s30, s31, s32)
    v3 = (v30, v31, v32)
    x, y, z, c = place()
    zl = z % 2
    sib = device(x, y, z, 1 - c)
    pieces = range(3)
    yz = ((1 - c, c), (1 - c, c), (c, 1 - c))

    def pos(p):
        m, n = yz[p]
        if p == 0:
            return y * m + z * n, z * m + y * n, x
        return x, z * m + y * n, y * m + z * n

    def coords(p, p1, p2, p3):
        m, n = yz[p]
        if p == 0:
            return p3, p1 * m + p2 * n, p2 * m + p1 * n
        return p1, p3 * m + p2 * n, p2 * m + p3 * n

    def peer(p, d1, d2, d3):
        p1, p2, p3 = pos(p)
        return device(*coords(p, (p1 + d1) % 4, (p2 + d2) % 4, (p3 + d3) % 4), c)

    def wslot(p, a3, a2_, start, n):
        if p == 0:
            return wgp.at[a2_, pl.ds(start, n), a3]
        bx, by, bz = coords(p, 0, a2_, a3)
        if p == 1:
            return wgn.at[bz % 2, by, bz // 2, pl.ds(start, n)]
        return wgn.at[2, by, bz // 2, pl.ds(start, n), :, pl.ds(pl.multiple_of((bz % 2) * 128, 128), 128)]

    def remote(src, dst, ss, rs, dev):
        return pltpu.make_async_remote_copy(
            src_ref=src, dst_ref=dst, send_sem=ss, recv_sem=rs, device_id=dev, device_id_type=MESH
        )

    mine = pl.ds(pl.multiple_of(c * HC, 128), HC)
    theirs = pl.ds(pl.multiple_of((1 - c) * HC, 128), HC)
    inputs = [
        pltpu.make_async_copy(src, dst, small.at[i])
        for i, (src, dst) in enumerate(
            (
                (w_hbm, w_ref),
                (cnt_hbm, cnt_ref),
                (ref_hbm, ref_ref),
                (lw_hbm, lw_ref),
                (seg_hbm, seg_ref),
                (gain_hbm, gain_in),
            )
        )
    ]
    for copy in inputs:
        copy.start()
    loads = [
        pltpu.make_async_copy(a_hbm, a2.at[0], loc.at[0]),
        pltpu.make_async_copy(t_hbm.at[:, mine], t2.at[0], loc.at[1]),
        pltpu.make_async_copy(r_hbm.at[:, mine], r2.at[0], loc.at[2]),
    ]
    for copy in loads:
        copy.start()

    partners = [sib, device(x, y, z + 1 - 2 * zl, 1 - c)]
    for d in (1, 2, 3):
        partners.append(device((x + d) % 4, y, z, c))
        partners.append(device(x, (y + d) % 4, z, c))
        partners.append(device(x, y, (z + d) % 4, c))
    barrier = pltpu.get_barrier_semaphore()
    for q in partners:
        pl.semaphore_signal(barrier, inc=1, device_id=q, device_id_type=MESH)

    for copy in inputs:
        copy.wait()
    lane = lax.broadcasted_iota(jnp.int32, (1, CAP), 1)
    live = lane < cnt_ref[...].reshape(1, 1)
    weight = jnp.where(live, lw_ref[...], 0).astype(F32)
    magnitude = jnp.sum(jnp.abs(weight), axis=1, keepdims=True)
    rows8 = lax.broadcasted_iota(jnp.int32, (8, CAP), 0)
    meta[0] = jnp.where(
        rows8 == 0,
        jnp.broadcast_to(ref_ref[...], (8, CAP)),
        jnp.where(
            rows8 == 1,
            jnp.broadcast_to(weight, (8, CAP)),
            jnp.where(
                rows8 == 2,
                jnp.broadcast_to(seg_ref[...].astype(F32), (8, CAP)),
                jnp.broadcast_to(magnitude, (8, CAP)),
            ),
        ),
    )

    def shard_columns(core):
        base = core * HC
        return jnp.concatenate(
            [
                w_ref[:, pl.ds(pl.multiple_of(base + zl * 256, 128), 256)].astype(F32),
                w_ref[:, pl.ds(pl.multiple_of(base + 512 + zl * 256, 128), 256)].astype(F32),
                w_ref[:, pl.ds(pl.multiple_of(base + 1024 + zl * 128, 128), 128)].astype(F32),
            ],
            axis=1,
        )

    wx[0] = shard_columns(1 - c)
    gain_row[0, :] = gain_in[...]
    pl.semaphore_wait(barrier, len(partners))

    sib_w = remote(wx.at[0], wx.at[1], sib_s.at[0], sib_r.at[0], sib)
    sib_m = remote(meta.at[0], meta.at[1], sib_s.at[1], sib_r.at[1], sib)
    sib_a = remote(a_hbm, a2.at[1], sib_s.at[2], sib_r.at[2], sib)
    sib_t = remote(t_hbm.at[:, theirs], t2.at[1], sib_s.at[3], sib_r.at[3], sib)
    sib_res = remote(r_hbm.at[:, theirs], r2.at[1], sib_s.at[4], sib_r.at[4], sib)
    for copy in (sib_w, sib_m, sib_a, sib_t, sib_res):
        copy.start()

    own_w = shard_columns(c)
    sib_w.wait_recv()
    got_w = wx[1]
    first = c == 0
    block = jnp.concatenate(
        [jnp.where(first, own_w, got_w), jnp.where(first, got_w, own_w)], axis=0
    ).astype(BF16)
    bx0, by0, bz0 = x, y, z // 2
    wgp[pos(0)[1], pos(0)[0], x] = block[:, 0:256]
    wgn[zl, by0, bz0, bx0] = block[:, 256:512]
    wgn[2, by0, bz0, bx0, :, pl.ds(pl.multiple_of(zl * 128, 128), 128)] = block[:, 512:640]

    ph1, ph2, ph2r, ph3, ph4 = {}, {}, {}, {}, {}
    for p in pieces:
        p1, p2, p3 = pos(p)
        for d in (1, 2, 3):
            slot = wslot(p, p3, p2, p1, 1)
            ph1[p, d] = remote(slot, slot, p1_s.at[p, d - 1], p1_r.at[p, d - 1], peer(p, d, 0, 0))
        line = wslot(p, p3, p2, 0, 4)
        low = wslot(p, p3, (p2 + 3) % 4, 0, 2)
        high = wslot(p, p3, (p2 + 1) % 4, 2, 2)
        ph2[p, 1] = remote(line, line, p2_s.at[p, 0], p2_r.at[p, 0], peer(p, 0, 1, 0))
        ph2[p, 3] = remote(line, line, p2_s.at[p, 1], p2_r.at[p, 1], peer(p, 0, 3, 0))
        ph2r[p, 1] = remote(low, low, p2_s.at[p, 2], p2_r.at[p, 2], peer(p, 0, 1, 0))
        ph2r[p, 3] = remote(high, high, p2_s.at[p, 3], p2_r.at[p, 3], peer(p, 0, 3, 0))
        for d in range(4):
            a2_ = (p2 + d) % 4
            line = wslot(p, p3, a2_, 0, 4)
            low = wslot(p, (p3 + 3) % 4, a2_, 0, 2)
            high = wslot(p, (p3 + 1) % 4, a2_, 2, 2)
            ph3[p, d, 0] = remote(line, line, p3_s.at[p, d, 0], p3_r.at[p, d, 0], peer(p, 0, 0, 1))
            ph3[p, d, 1] = remote(line, line, p3_s.at[p, d, 1], p3_r.at[p, d, 1], peer(p, 0, 0, 3))
            ph4[p, d, 0] = remote(low, low, p4_s.at[p, d, 0], p4_r.at[p, d, 0], peer(p, 0, 0, 1))
            ph4[p, d, 1] = remote(high, high, p4_s.at[p, d, 1], p4_r.at[p, d, 1], peer(p, 0, 0, 3))

    sends = [sib_w, sib_m, sib_a, sib_t, sib_res]

    def start(copy):
        copy.start()
        sends.append(copy)

    def den_phase(axis, value):
        at_ = (x, y, z)[axis]
        den[axis, at_] = value
        copies = []
        for d in (1, 2, 3):
            q = [x, y, z]
            q[axis] = (at_ + d) % 4
            slot = den.at[axis, at_]
            copy = remote(
                slot, slot, den_s.at[axis, d - 1], den_r.at[axis, d - 1], device(q[0], q[1], q[2], c)
            )
            start(copy)
            copies.append(copy)
        return copies

    def den_total(axis, copies):
        for copy in copies:
            copy.wait_recv()
        return den[axis, 0] + den[axis, 1] + den[axis, 2] + den[axis, 3]

    sib_m.wait_recv()
    den_copies = den_phase(0, meta[0, :, 0:128] * 0 + (meta[0, 3:4, 0:128] + meta[1, 3:4, 0:128]))
    for d in (1, 3, 2):
        for p in pieces:
            start(ph1[p, d])

    def transpose_rows(slot):
        @pl.loop(0, DW // 128)
        def _(k):
            off = pl.ds(pl.multiple_of(k * 128, 128), 128)
            at[off, slot * CAP : (slot + 1) * CAP] = a2[slot, :, off].T

    def transpose_targets(slot):
        @pl.loop(0, NG)
        def _(g):
            for k in (0, 1):
                off = pl.ds(pl.multiple_of(g * GW + k * 128, 128), 128)
                tt[g, k * 128 : (k + 1) * 128, slot * CAP : (slot + 1) * CAP] = t2[slot, :, off].T

    def slabs(p, v, h):
        m, n = yz[p]
        rows, weights = [], []
        if p == 0:
            for yy in range(4):
                for zz in range(2):
                    zc = 2 * zz + h
                    rows.append(at[pl.ds(pl.multiple_of(((yy * 2 + zz) * 4 + v) * ROW, 16), ROW), :])
                    weights.append(wgp[zc * m + yy * n, yy * m + zc * n, v])
            side = h
        else:
            side = h * m + (v % 2) * n
            for k in (0, 1):
                by = v * m + (2 * k + h) * n
                bz = k * m + (v // 2) * n
                rows.append(at[pl.ds(pl.multiple_of((by * 2 + bz) * 4 * ROW, 16), 4 * ROW), :])
                if p == 1:
                    weights.append(wgn[side, by, bz].reshape(4 * ROW, GW))
                else:
                    part = wgn[2, by, bz, :, :, pl.ds(pl.multiple_of(side * 128, 128), 128)]
                    weights.append(part.reshape(4 * ROW, 128))
        return jnp.concatenate(rows, axis=0), jnp.concatenate(weights, axis=0), side

    def forward(p, v, only=None):
        @pl.loop(0 if only is None else only, 2 if only is None else only + 1)
        def _(h):
            rows, weights, side = slabs(p, v, h)
            res = lax.dot_general(weights, rows, (((0,), (0,)), ((), ())), preferred_element_type=F32)
            if p == 0:
                pr[side] += res
            elif p == 1:
                pr[2 + side] += res
            else:
                pr[4, pl.ds(pl.multiple_of(side * 128, 128), 128)] += res

    def near(p, d, odd):
        forward(p, last_place(p, d), (pos(p)[1] + odd) % 2)

    def last_place(p, d):
        return (pos(p)[2] + d) % 4

    gcol[...] = jnp.broadcast_to(
        gain_row[:, pl.ds(pl.multiple_of(c * HC, 128), HC)], (128, HC)
    ).T.reshape(NG, GW, 128)

    @pl.loop(0, NG)
    def _(g):
        pr[g] = jnp.zeros((GW, 2 * CAP), F32)

    for copy in loads:
        copy.wait()

    den_copies = [den_copies]

    def spread_own(p):
        for d in (1, 3, 2):
            ph1[p, d].wait_recv()
        if p == 0:
            den_copies.append(den_phase(1, den_total(0, den_copies[0])))
        for d in (1, 3):
            start(ph2[p, d])

    def spread(p, d):
        if d == 2:
            ph2r[p, 1].wait_recv()
            ph2r[p, 3].wait_recv()
        else:
            ph2[p, 4 - d].wait_recv()
            start(ph2r[p, 4 - d])
        start(ph3[p, d, 0])
        start(ph3[p, d, 1])

    def relay(p, d):
        for s in (0, 1):
            ph3[p, d, s].wait_recv()
            start(ph4[p, d, s])

    stat[...] = jnp.zeros((2, 8, 2 * CAP), F32)

    def token_sums(low, high):
        @pl.loop(low, high)
        def _(g):
            for slot in (0, 1):
                cols = slice(slot * CAP, (slot + 1) * CAP)
                gains = jnp.concatenate([gcol[g]] * 4, axis=1)
                p_ = pr[g, :, cols]
                stat[0, :, cols] += jnp.sum((p_ * p_).reshape(GW // 8, 8, CAP), axis=0)
                tp = p_ * tt[g, :, cols].astype(F32) * gains
                stat[1, :, cols] += jnp.sum(tp.reshape(GW // 8, 8, CAP), axis=0)

    def arrived(p, steps):
        for d in steps:
            for s in (0, 1):
                ph4[p, d, s].wait_recv()

    transpose_rows(0)
    spread_own(0)
    start(ph3[0, 0, 0])
    start(ph3[0, 0, 1])
    spread_own(1)
    spread_own(2)
    start(ph3[2, 0, 0])
    start(ph3[2, 0, 1])
    sib_a.wait_recv()
    transpose_rows(1)
    spread(0, 3)
    spread(0, 1)
    spread(2, 3)
    sib_t.wait_recv()
    transpose_targets(0)
    transpose_targets(1)
    spread(2, 1)
    sib_res.wait_recv()
    for slot in (0, 1):
        part = jnp.zeros((CAP, 128), F32)
        for k in range(HC // 128):
            cols = slice(k * 128, (k + 1) * 128)
            part += t2[slot, :, cols].astype(F32) * r2[slot, :, cols].astype(F32)
        sp[0, slot] = jnp.broadcast_to(jnp.sum(part.T, axis=0, keepdims=True), (8, CAP))
    spread(1, 1)
    spread(0, 2)
    relay(2, 1)
    relay(2, 0)
    relay(2, 3)
    spread(2, 2)
    spread(1, 3)
    den_copies = den_phase(2, den_total(1, den_copies[1]))
    relay(0, 3)
    forward(2, last_place(2, 0))
    forward(0, last_place(0, 0))
    relay(0, 1)
    near(2, 3, 1)
    spread(1, 2)
    relay(2, 2)
    forward(1, last_place(1, 0))
    relay(0, 2)
    relay(0, 0)
    arrived(2, (1, 3))
    near(2, 2, 1)
    near(2, 1, 1)
    start(ph3[1, 0, 0])
    start(ph3[1, 0, 1])
    forward(0, last_place(0, 1))
    relay(1, 1)
    relay(1, 3)
    near(2, 3, 0)
    arrived(2, (0, 2))
    near(2, 2, 0)
    near(2, 1, 0)
    token_sums(4, NG)
    relay(1, 2)
    forward(0, last_place(0, 3))
    near(1, 3, 1)
    relay(1, 0)
    near(1, 1, 1)
    near(1, 3, 0)
    near(1, 1, 0)
    arrived(1, (1, 3))
    near(1, 2, 1)
    arrived(0, ORDER)
    forward(0, last_place(0, 2))
    token_sums(0, 2)
    arrived(1, (0, 2))
    near(1, 2, 0)
    denominator = jnp.maximum(den_total(2, den_copies)[0:1, 0:1], 1.0)
    token_sums(2, 4)

    row = lax.broadcasted_iota(jnp.int32, (8, CAP), 0)
    for slot in (0, 1):
        cols = slice(slot * CAP, (slot + 1) * CAP)
        q1 = jnp.sum(stat[0, :, cols], axis=0, keepdims=True)
        q3 = jnp.sum(stat[1, :, cols], axis=0, keepdims=True)
        sp[0, slot] = jnp.where(row == 0, q1, jnp.where(row == 1, q3, sp[0, slot]))

    swap = [
        remote(sp.at[0, s], sp.at[1, 1 - s], sib_s.at[5 + s], sib_r.at[5 + s], sib) for s in (0, 1)
    ]
    for copy in swap:
        start(copy)
    for copy in swap:
        copy.wait_recv()

    segs = lax.broadcasted_iota(jnp.int32, (SEGS, CAP), 0).astype(F32)
    for slot in (0, 1):
        total = sp[0, slot] + sp[1, slot]
        q1, q3, q2 = total[0:1], total[1:2], total[2:3]
        scale = jnp.sqrt(q1 * (1.0 / DW) + 1e-06)
        score = q2 + q3 / scale
        ref, wgt, seg = meta[slot, 0:1], meta[slot, 1:2], meta[slot, 2:3]
        forget = jnp.maximum(-wgt, 0.0)
        retain = jnp.maximum(wgt, 0.0)
        table = (seg == segs).astype(F32)
        seg_sum = jnp.sum(table * (forget * (score - ref)), axis=1, keepdims=True)
        has = jnp.sum(table * forget, axis=1, keepdims=True) > 0.5
        scaled = npo_beta * seg_sum
        if slot == 0:
            soft = jnp.maximum(scaled, 0.0) + jnp.log1p(jnp.exp(-jnp.abs(scaled)))
            npo = jnp.sum(jnp.where(has, 2.0 / npo_beta * soft, 0.0), axis=0, keepdims=True)
            loss = npo - jnp.sum(retain * score, axis=1, keepdims=True)
            gsum[0, x, 0:1, HC : HC + 128] = jnp.broadcast_to(loss, (1, 128))
        sig = jnp.sum(table * jax.nn.sigmoid(scaled), axis=0, keepdims=True)
        grad = loss_scale / denominator * (forget * 2.0 * sig - retain)
        alpha[slot] = jnp.broadcast_to(grad / scale, (8, CAP))
        beta[slot] = jnp.broadcast_to(q3 / (scale * scale * DW), (8, CAP))

    def gradient(low, high):
        @pl.loop(low, high)
        def _(g):
            gains = jnp.concatenate([gcol[g]] * 4, axis=1)
            part = jnp.zeros((GW, 128), F32)
            for slot in (0, 1):
                cols = slice(slot * CAP, (slot + 1) * CAP)
                al, be = alpha[slot, 0:1], beta[slot, 0:1]
                p_ = pr[g, :, cols]
                t = tt[g, :, cols].astype(F32)
                pg[g, :, cols] = (al * (t * gains - p_ * be)).astype(BF16)
                u = al * t * p_
                part += (u[:, 0:128] + u[:, 128:256]) + (u[:, 256:384] + u[:, 384:512])
            gacc[g] = part

    def grad_blocks(p, v, emit):
        m, n = yz[p]
        for h in (0, 1):
            rows, _, side = slabs(p, v, h)
            if p == 2:
                right = pg[4, pl.ds(pl.multiple_of(side * 128, 128), 128)]
            else:
                right = pg[2 * p + side]
            res = lax.dot_general(rows, right, (((1,), (1,)), ((), ())), preferred_element_type=F32)
            for k in range(8):
                value = res[k * ROW : (k + 1) * ROW]
                if p == 0:
                    yy, zc = k // 2, 2 * (k % 2) + h
                    emit(zc * m + yy * n, yy * m + zc * n, value)
                else:
                    emit(2 * (k // 4) + h, k % 4, value)

    q0, qa, q1, q2, q2r, q3 = {}, {}, {}, {}, {}, {}
    for p in pieces:
        p1, p2, p3 = pos(p)
        for s in (0, 1):
            half = pl.ds(2 * s, 2)
            to = peer(p, 0, 0, 1 + 2 * s)
            q0[p, s] = remote(st_o[p].at[:, half], rl[p].at[s], q0_s.at[p, s], q0_r.at[p, s], to)
            free = pl.ds(2 * (1 - s), 2)
            for d in range(4):
                i = (p2 + d) % 4
                qa[p, s, d] = remote(
                    st_n[p].at[s, i, free], rv[p].at[s, i, free], qa_s.at[p, s, d], qa_r.at[p, s, d], to
                )
                q1[p, s, d] = remote(
                    st_n[p].at[s, i, half], rv[p].at[s, i, half], q1_s.at[p, s, d], q1_r.at[p, s, d], to
                )
        for t_ in (0, 1):
            to = peer(p, 0, 1 + 2 * t_, 0)
            q2[p, 1 + 2 * t_] = remote(
                s2[p].at[2 * t_], v2[p].at[t_], q2_s.at[p, t_], q2_r.at[p, t_], to
            )
            q2r[p, t_] = remote(
                s2[p].at[1, pl.ds(2 * t_, 2)], w2[p].at[t_], q2_s.at[p, 2 + t_], q2_r.at[p, 2 + t_], to
            )
        for d in (1, 2, 3):
            q3[p, d] = remote(
                s3[p].at[d - 1], v3[p].at[d - 1], q3_s.at[p, d - 1], q3_r.at[p, d - 1], peer(p, d, 0, 0)
            )

    def put(ref, prefix=()):
        def emit(i, j, value):
            ref[prefix + (i, j)] = value.astype(ref.dtype)

        return emit

    def gain_phase(axis):
        at_ = (x, y, z)[axis]
        copies = []
        for d in (1, 2, 3):
            q = [x, y, z]
            q[axis] = (at_ + d) % 4
            slot = gsum.at[axis, at_]
            copy = remote(
                slot, slot, g_s.at[axis, d - 1], g_r.at[axis, d - 1], device(q[0], q[1], q[2], c)
            )
            start(copy)
            copies.append(copy)
        return copies

    def gain_total(axis, copies):
        for copy in copies:
            copy.wait_recv()
        return (gsum[axis, 0] + gsum[axis, 1]) + (gsum[axis, 2] + gsum[axis, 3])

    waited = set()

    def await_once(name, copy):
        if name not in waited:
            waited.add(name)
            copy.wait_recv()

    def first_blocks(p):
        grad_blocks(p, (pos(p)[2] + 2) % 4, put(st_o[p]))
        start(q0[p, 0])
        start(q0[p, 1])

    def near_blocks(p, t_):
        grad_blocks(p, (pos(p)[2] + 1 + 2 * t_) % 4, put(st_n[p], (t_,)))
        start(qa[p, t_, 2])
        start(qa[p, t_, 1])

    def relay_sum(p, d):
        i = (pos(p)[1] + d) % 4
        for t_ in (0, 1):
            await_once(("q0", p, t_), q0[p, t_])
            half = slice(2 * t_, 2 * t_ + 2)
            both = st_n[p][t_, i, half].astype(F32) + rl[p][t_, i].astype(F32)
            st_n[p][t_, i, half] = both.astype(BF16)
            start(q1[p, t_, d])
            if d in (1, 3):
                start(qa[p, t_, 3 if d == 1 else 0])

    def lines(h, yy):
        m, n = yz[0]
        out = []
        for zz in range(2):
            zc = 2 * zz + h
            out.append(wgp[zc * m + yy * n, yy * m + zc * n].reshape(4 * ROW, GW))
        return jnp.concatenate(out, axis=0)

    def grad_rows(slot, yy):
        res = jnp.zeros((640, CAP), F32)
        for g in range(NG):
            w = lines(g, yy) if g < 2 else wgn[g - 2, yy].reshape(640, GW)
            right = pg[g, :, slot * CAP : (slot + 1) * CAP]
            res = res + jnp.dot(w, right, preferred_element_type=F32)
        return res

    ga_copies = {}

    def sibling_rows(yy):
        rows = slice(yy * 640, (yy + 1) * 640)
        ga_send[rows, :] = grad_rows(1, yy).astype(BF16)
        copy = remote(ga_send.at[rows], ga_recv.at[rows], ga_s.at[yy], ga_r.at[yy], sib)
        start(copy)
        ga_copies[yy] = copy

    ga_stores = []

    def own_rows(yy):
        ga_copies[yy].wait_recv()
        rows = slice(yy * 640, (yy + 1) * 640)
        both = (grad_rows(0, yy) + ga_recv[rows, :].astype(F32)).astype(BF16)
        for k in range(5):
            ga_own[:, yy * 640 + k * 128 : yy * 640 + (k + 1) * 128] = both[k * 128 : (k + 1) * 128].T
        copy = pltpu.make_async_copy(ga_own.at[:, rows], ga_out.at[:, rows], loc.at[3 + yy])
        copy.start()
        ga_stores.append(copy)

    def reduce_step(p, d):
        p1, p2, p3 = pos(p)
        i = (p2 + d) % 4
        for t_ in (0, 1):
            qa[p, t_, d].wait_recv()
            q1[p, t_, d].wait_recv()
        total = own[p][i] + rv[p][0, i].astype(F32) + rv[p][1, i].astype(F32)
        if d == 0:
            own[p][i] = total
            return
        s2[p][d - 1] = total.astype(BF16)
        if d == 2:
            start(q2r[p, 0])
            start(q2r[p, 1])
            return
        t_ = d // 2
        half = slice(2 * t_, 2 * t_ + 2)
        q2r[p, t_].wait_recv()
        s2[p][d - 1, half] = (total[half] + w2[p][t_].astype(F32)).astype(BF16)
        start(q2[p, d])

    def second(p):
        p1, p2, p3 = pos(p)
        acc = own[p][p2]
        for t_ in (0, 1):
            q2[p, 1 + 2 * t_].wait_recv()
            acc = acc + v2[p][t_].astype(F32)
        own[p][p2] = acc
        for d in (1, 3, 2):
            s3[p][d - 1] = own[p][p2, (p1 + d) % 4].astype(BF16)
            start(q3[p, d])

    offs = (0, 256, 512)
    zn = z + 1 - 2 * zl
    last = {}

    def third(p):
        p1, p2, p3 = pos(p)
        acc = own[p][p2, p1]
        for d in (1, 3, 2):
            q3[p, d].wait_recv()
            acc = acc + v3[p][d - 1].astype(F32)
        cols = slice(offs[p], offs[p] + WIDTH[p])
        pad = jnp.zeros((PAD - HALF, WIDTH[p]), F32)
        for core in (0, 1):
            part = acc[core * HALF : (core + 1) * HALF]
            fb[core, :, cols] = jnp.concatenate([part, pad], axis=0).astype(BF16)
        mine_ = fb.at[c, :, cols]
        other = fb.at[1 - c, :, cols]
        last[p] = [
            remote(other, fr.at[0, :, cols], qf_s.at[p, 0], qf_r.at[p, 0], sib),
            remote(mine_, fr.at[1, :, cols], qf_s.at[p, 1], qf_r.at[p, 1], device(x, y, zn, c)),
            remote(other, fr.at[2, :, cols], qf_s.at[p, 2], qf_r.at[p, 2], device(x, y, zn, 1 - c)),
        ]
        for copy in (last[p][1], last[p][2], last[p][0]):
            start(copy)

    gradient(2, 4)
    first_blocks(1)
    gradient(0, 2)
    first_blocks(0)
    gradient(4, NG)
    first_blocks(2)

    @pl.loop(0, NG)
    def _(g):
        cols = pl.ds(pl.multiple_of(g * GW, GW), GW)
        gsum[0, x, 0:1, cols] = jnp.sum(gacc[g].T, axis=0, keepdims=True)

    gain_copies = gain_phase(0)
    near_blocks(0, 1)
    near_blocks(1, 0)
    near_blocks(2, 0)
    near_blocks(1, 1)
    near_blocks(2, 1)
    grad_blocks(2, pos(2)[2], put(own[2]))
    relay_sum(1, 2)
    relay_sum(2, 2)
    near_blocks(0, 0)
    relay_sum(2, 1)
    relay_sum(0, 2)
    relay_sum(1, 1)
    sibling_rows(0)
    reduce_step(2, 2)
    grad_blocks(1, pos(1)[2], put(own[1]))
    relay_sum(1, 3)
    reduce_step(1, 2)
    relay_sum(0, 1)
    relay_sum(2, 3)
    grad_blocks(0, pos(0)[2], put(own[0]))
    relay_sum(1, 0)
    sibling_rows(3)
    sibling_rows(2)
    sibling_rows(1)
    relay_sum(0, 3)
    relay_sum(2, 0)
    reduce_step(0, 2)
    reduce_step(1, 1)
    gsum[1, y] = gain_total(0, gain_copies)
    gain_copies = gain_phase(1)
    reduce_step(1, 3)
    own_rows(0)
    reduce_step(1, 0)
    reduce_step(2, 1)
    reduce_step(2, 3)
    relay_sum(0, 0)
    reduce_step(0, 1)
    reduce_step(0, 3)
    second(1)
    gsum[2, z] = gain_total(1, gain_copies)
    gain_copies = gain_phase(2)
    own_rows(2)
    reduce_step(2, 0)
    second(2)
    reduce_step(0, 0)
    second(0)
    third(1)
    third(2)
    total = gain_total(2, gain_copies)
    gsib[c] = total
    gcopy = remote(gsib.at[c], gsib.at[c], sib_s.at[8], sib_r.at[8], sib)
    start(gcopy)
    third(0)
    own_rows(3)
    own_rows(1)

    def place_columns(core, side, value):
        base = core * HC
        value = value.astype(F32)[0:HALF]
        gw_out[:, pl.ds(pl.multiple_of(base + side * 256, 128), 256)] = value[:, 0:256]
        gw_out[:, pl.ds(pl.multiple_of(base + 512 + side * 256, 128), 256)] = value[:, 256:512]
        gw_out[:, pl.ds(pl.multiple_of(base + 1024 + side * 128, 128), 128)] = value[:, 512:640]

    place_columns(c, zl, fb[c])

    gcopy.wait_recv()
    gg_out[...] = jnp.concatenate([gsib[0, 0, 0:HC], gsib[1, 0, 0:HC]], axis=0)
    loss_out[...] = (gsib[0, 0:1, HC : HC + 1] + gsib[1, 0:1, HC : HC + 1]) / denominator

    for p in (1, 2, 0):
        for copy in last[p]:
            copy.wait_recv()
    place_columns(1 - c, zl, fr[0])
    place_columns(c, 1 - zl, fr[1])
    place_columns(1 - c, 1 - zl, fr[2])

    for copy in sends:
        copy.wait_send()
    for copy in ga_stores:
        copy.wait()


def scratch():
    dma = pltpu.SemaphoreType.DMA
    vm = pltpu.VMEM
    out = [
        vm((1, CAP), F32),
        vm((1, CAP), jnp.int32),
        vm((1, CAP), jnp.int32),
        vm((1,), jnp.int32),
        vm((HALF, DW), BF16),
        vm((DW,), F32),
        dma((6,)),
        vm((1, DW), F32),
        vm((NG, GW, 128), F32),
        vm((2, CAP, DW), BF16),
        vm((DW, 2 * CAP), BF16),
        vm((2, CAP, HC), BF16),
        vm((2, CAP, HC), BF16),
        vm((NG, GW, 2 * CAP), BF16),
        vm((4, 4, 4, ROW, GW), BF16),
        vm((NG - 2, 4, 2, 4, ROW, GW), BF16),
        vm((NG, GW, 2 * CAP), F32),
        vm((NG, GW, 2 * CAP), BF16),
        vm((2, HALF, 640), F32),
        vm((2, 8, CAP), F32),
        vm((2, 8, 2 * CAP), F32),
        vm((2, 2, 8, CAP), F32),
        vm((2, 8, CAP), F32),
        vm((2, 8, CAP), F32),
        vm((NG, GW, 128), F32),
        vm((3, 4, 8, 128), F32),
        vm((3, 4, 1, HC + 128), F32),
        vm((2, 1, HC + 128), F32),
    ]
    out += [vm((4, 4, ROW, w), BF16) for w in WIDTH]
    out += [vm((2, 4, 4, ROW, w), BF16) for w in WIDTH]
    out += [vm((2, 4, 2, ROW, w), BF16) for w in WIDTH]
    out += [vm((2, 4, 4, ROW, w), BF16) for w in WIDTH]
    out += [vm((4, 4, ROW, w), F32) for w in WIDTH]
    out += [vm((3, 4, ROW, w), BF16) for w in WIDTH]
    out += [vm((2, 4, ROW, w), BF16) for w in WIDTH]
    out += [vm((2, 2, ROW, w), BF16) for w in WIDTH]
    out += [vm((3, ROW, w), BF16) for w in WIDTH]
    out += [vm((3, ROW, w), BF16) for w in WIDTH]
    out += [
        vm((2, PAD, 640), BF16),
        vm((3, PAD, 640), BF16),
        vm((DW, CAP), BF16),
        vm((DW, CAP), BF16),
        vm((CAP, DW), BF16),
        dma((7,)),
    ]
    for shape in (
        (9,), (3, 3), (3, 3), (3, 3), (3, 4), (3, 4, 2), (3, 4, 2),
        (3, 2), (3, 2, 4), (3, 2, 4), (3, 4), (3, 3), (3, 3), (4,),
    ):
        out += [dma(shape), dma(shape)]
    return out


def finish(gw, gg, ga, loss, gw_out, gg_out, ga_out, loss_out, gw_v, gg_v, ga_v, loss_v, s_in, s_out):
    n = CAP // PARTS
    trips = []
    for k in range(PARTS):
        rows = slice(k * n, (k + 1) * n)
        trips.append((ga.at[rows], ga_v.at[rows], ga_out.at[rows]))
    trips += [(gw, gw_v, gw_out), (gg, gg_v, gg_out), (loss, loss_v, loss_out)]
    loads = [pltpu.make_async_copy(src, mid, s_in.at[i]) for i, (src, mid, _) in enumerate(trips)]
    stores = [pltpu.make_async_copy(mid, dst, s_out.at[i]) for i, (_, mid, dst) in enumerate(trips)]
    for copy in loads:
        copy.start()
    for load, store in zip(loads, stores):
        load.wait()
        store.start()
    for copy in stores:
        copy.wait()


def shards(attention_out, residual, target_rows, ref_logit, loss_weight, segment, counts, out_weight, norm_gain):
    any_ = pl.BlockSpec(memory_space=pl.ANY)
    vmem = pl.BlockSpec(memory_space=pltpu.VMEM)
    gw, gg, ga, loss = pl.pallas_call(
        kernel,
        out_shape=(
            jax.ShapeDtypeStruct((HALF, DW), F32),
            jax.ShapeDtypeStruct((DW,), F32),
            jax.ShapeDtypeStruct((CAP, DW), BF16),
            jax.ShapeDtypeStruct((1, 1), F32),
        ),
        in_specs=[any_] * 9,
        out_specs=(vmem, vmem, any_, vmem),
        scratch_shapes=scratch(),
        compiler_params=pltpu.CompilerParams(
            collective_id=0, has_side_effects=True, vmem_limit_bytes=62 * 2**20
        ),
        cost_estimate=pl.CostEstimate(
            flops=3 * 2 * CAP * DW * DW, bytes_accessed=4 * CAP * DW * 2, transcendentals=0
        ),
    )(
        attention_out,
        residual,
        target_rows,
        ref_logit,
        loss_weight,
        segment,
        counts,
        out_weight,
        norm_gain,
    )
    gw, gg, ga, loss = pl.pallas_call(
        finish,
        out_shape=(
            jax.ShapeDtypeStruct((HALF, DW), F32),
            jax.ShapeDtypeStruct((DW,), F32),
            jax.ShapeDtypeStruct((CAP, DW), BF16),
            jax.ShapeDtypeStruct((1, 1), F32),
        ),
        in_specs=[any_] * 4,
        out_specs=(any_,) * 4,
        scratch_shapes=[
            pltpu.VMEM((HALF, DW), F32),
            pltpu.VMEM((DW,), F32),
            pltpu.VMEM((CAP, DW), BF16),
            pltpu.VMEM((1, 1), F32),
            pltpu.SemaphoreType.DMA((PARTS + 3,)),
            pltpu.SemaphoreType.DMA((PARTS + 3,)),
        ],
        compiler_params=pltpu.CompilerParams(vmem_limit_bytes=62 * 2**20),
    )(gw, gg, ga, loss)
    return gw, gg, ga, loss[0, 0]


def solution(mesh):
    rows = P(("dp", "fsdp"), None)
    placed = (rows,) * 6 + (P(("dp", "fsdp")), P("fsdp", None), P())
    return jax.shard_map(
        shards,
        mesh=mesh,
        in_specs=placed,
        out_specs=(P("fsdp", None), P(), rows, P()),
        check_vma=False,
    )
```
